256 devices in a mesh: seq: 64 (over z, y, core), head: 4 (over x).
Axes of the slice: x: 4, y: 4, z: 8, core: 2. Of those that a mesh axis runs over, the one named last changes fastest.
Arguments:
- query_latent: bfloat16 [16384, 128, 576], P('seq', 'head'), may hold values from -16 to 16
- stretch_latent: bfloat16 [16384, 576], P('seq'), may hold values from -8 to 8
- cache_latent: bfloat16 [32768, 576], P('seq'), may hold values from -8 to 8
- query_index: bfloat16 [16384, 64, 128], P('seq', 'head'), may hold values from -8 to 8
- stretch_index: bfloat16 [16384, 128], P('seq'), may hold values from -8 to 8
- cache_index: bfloat16 [32768, 128], P('seq'), may hold values from -8 to 8
- index_gains: float32 [16384, 64], P('seq', 'head'), may hold values from -0.15 to 0.15
- block_ids: int32 [256, 7], P('seq'), may hold values from 0 to 511, as said below
Outputs:
- divergence: float32 [16384], P('seq')
- query_index_grad: bfloat16 [16384, 64, 128], P('seq', 'head')
- index_gains_grad: float32 [16384, 64], P('seq', 'head')
- cache_index_grad: float32 [32768, 128], P('seq')
- stretch_index_grad: float32 [16384, 128], P('seq')
The draws below stay inside these ranges and needn't reach their ends.
Inputs may be any that keep to these rules, and one draw needn't show every extreme that they name: `block_ids`: the 7 entries of a row are distinct cached blocks. Over the 4 consecutive rows starting at a multiple of 4, at most 1 entries name blocks of one group o*8 to o*8 + 7, those entries are distinct, and some group is named exactly 1 times.
All inputs are finite; a program needn't handle non-finite values.
Results may differ from the reference program's by a relative error of at most 0.0065.
Values may be sent and summed in bfloat16 or wider, within the bound.
A program may use at most 128 MiB of HBM per device.

```python
import jax
import jax.numpy as jnp
from jax import lax

HEADS = 128
KDIM = 576
IHEADS = 64
IDIM = 128
BLK = 64
TOPB = 8
QB_DEV = 4
CB_DEV = 8
QUERIES = 16384
PREFIX = 32768
QBLOCKS = 256


def latent_common(key):
    first = jax.random.fold_in(key, 0)
    stretch = jax.random.normal(first, (QUERIES, KDIM), jnp.float32)
    return jnp.clip(stretch, -8.0, 8.0)


def index_common(key):
    first = jax.random.fold_in(key, 0)
    stretch = jax.random.normal(first, (QUERIES, IDIM), jnp.float32)
    return jnp.clip(stretch, -8.0, 8.0)


def draw_stretch_latent(key, part):
    stretch = latent_common(key)
    return stretch.astype(jnp.bfloat16)


def draw_query_latent(key, part):
    key = jax.random.fold_in(key, 7)
    first = jax.random.fold_in(key, 0)
    query_vectors = jax.random.normal(first, (QUERIES, HEADS, KDIM), jnp.float32)
    return jnp.clip(query_vectors, -16.0, 16.0).astype(jnp.bfloat16)


def draw_stretch_index(key, part):
    stretch = index_common(key)
    return stretch.astype(jnp.bfloat16)


def draw_query_index(key, part):
    key = jax.random.fold_in(key, 11)
    first = jax.random.fold_in(key, 0)
    query_vectors = jax.random.normal(first, (QUERIES, IHEADS, IDIM), jnp.float32)
    return jnp.clip(query_vectors, -8.0, 8.0).astype(jnp.bfloat16)


def draw_index_gains(key, part):
    key = jax.random.fold_in(key, 13)
    index_head_gains = jnp.clip(0.05 * jax.random.normal(key, (QUERIES, IHEADS), jnp.float32), -0.15, 0.15)
    return index_head_gains


def draw_block_ids(key, part):
    key = jax.random.fold_in(key, 5)
    first, second = jax.random.split(key)
    groups = QBLOCKS // QB_DEV
    slot_count = QB_DEV * (TOPB - 1)
    owner_perm = jax.vmap(lambda single: jax.random.permutation(single, groups))(jax.random.split(first, groups))
    local_perm = jax.vmap(lambda single: jax.random.permutation(single, CB_DEV))(jax.random.split(second, groups * groups))
    local_perm = local_perm.reshape(groups, groups, CB_DEV)
    slots = jnp.arange(slot_count)
    owners = owner_perm[:, slots % groups]
    ranks = slots // groups
    locals_chosen = local_perm[jnp.arange(groups)[:, None], owners, ranks[None, :]]
    chosen = owners * CB_DEV + locals_chosen
    return chosen.reshape(QBLOCKS, TOPB - 1).astype(jnp.int32)


def block_scale(rng, dims, pieces, least, largest):
    factor_of = 1.0
    for dim, parts in pieces:
        draws = jax.random.uniform(jax.random.fold_in(jax.random.fold_in(rng, 6), dim), (parts,), jnp.float32, least / len(pieces), largest / len(pieces))
        factor_of = factor_of * jnp.repeat(jnp.exp(draws), dims[dim] // parts).reshape((-1,) + (1,) * (len(dims) - 1 - dim))
    return factor_of


def bell_draw(stream_key, dims, spread, reach, cuts=(), kind=jnp.bfloat16):
    result = spread * jax.random.normal(stream_key, dims, jnp.float32)
    if cuts:
        result = result * block_scale(stream_key, dims, cuts, -0.22, 0.18)
    return jnp.clip(result, -reach, reach).astype(kind)


def setup_inputs(seed: int = 0) -> dict:
    splits = jax.random.split(jax.random.key(seed), 9)
    return {
        "query_latent": draw_query_latent(jax.random.fold_in(splits[8], 71), 0),
        "stretch_latent": draw_stretch_latent(jax.random.fold_in(splits[8], 71), 0),
        "cache_latent": bell_draw(splits[2], (PREFIX, KDIM), 1.0, 8.0, ((0, 64),)),
        "query_index": draw_query_index(jax.random.fold_in(splits[8], 71), 0),
        "stretch_index": draw_stretch_index(jax.random.fold_in(splits[8], 71), 0),
        "cache_index": bell_draw(splits[5], (PREFIX, IDIM), 1.0, 8.0, ((0, 64),)),
        "index_gains": draw_index_gains(jax.random.fold_in(splits[8], 71), 0),
        "block_ids": draw_block_ids(jax.random.fold_in(splits[8], 71), 0),
    }


score_scale = 192.0 ** -0.5


def attention_mass(scores, allowed):
    masked = jnp.where(jnp.expand_dims(allowed, -2), scores, -jnp.inf)
    row_max = jnp.max(masked, axis=-1, keepdims=True)
    shifted = jnp.exp(masked - row_max)
    attention = shifted / jnp.sum(shifted, axis=-1, keepdims=True)
    return jnp.sum(attention, axis=-2)


def kl_terms(mass_sum, logits, allowed):
    target = mass_sum / HEADS
    masked = jnp.where(allowed, logits, -jnp.inf)
    row_max = jnp.max(masked, axis=-1, keepdims=True)
    shifted = jnp.exp(masked - row_max)
    total = jnp.sum(shifted, axis=-1, keepdims=True)
    model = shifted / total
    log_model = jnp.where(allowed, masked - row_max - jnp.log(total), 0.0)
    safe_target = jnp.where(target > 0, target, 1.0)
    pointwise = jnp.where(allowed, target * (jnp.log(safe_target) - log_model), 0.0)
    divergence = jnp.sum(pointwise, axis=-1)
    logit_gradient = jnp.where(allowed, model - target, 0.0)
    return divergence, logit_gradient


def reference(query_latent, stretch_latent, cache_latent, query_index, stretch_index, cache_index, index_gains, block_ids):
    picked_count = TOPB - 1
    span = TOPB * BLK
    latent_blocks = cache_latent.reshape(PREFIX // BLK, BLK, KDIM)
    index_blocks = cache_index.reshape(PREFIX // BLK, BLK, IDIM)
    columns = jnp.arange(span)
    row_pos = jnp.arange(BLK)
    allowed = (columns[None, :] < picked_count * BLK) | (columns[None, :] - picked_count * BLK <= row_pos[:, None])

    def step(carry, qblock):
        picked = block_ids[qblock]
        start = (qblock * BLK).astype(jnp.int32)
        latent_key_rows = jnp.concatenate([latent_blocks[picked].reshape(picked_count * BLK, KDIM),
                                       lax.dynamic_slice_in_dim(stretch_latent, start, BLK, 0)], 0).astype(jnp.float32)
        query_vectors = lax.dynamic_slice_in_dim(query_latent, start, BLK, 0).astype(jnp.float32)
        scores = jnp.einsum("qhd,kd->qhk", query_vectors, latent_key_rows) * score_scale
        mass_sum = attention_mass(scores, allowed)
        indexer_key_rows = jnp.concatenate([index_blocks[picked].reshape(picked_count * BLK, IDIM),
                                      lax.dynamic_slice_in_dim(stretch_index, start, BLK, 0)], 0).astype(jnp.float32)
        indexer_query_rows = lax.dynamic_slice_in_dim(query_index, start, BLK, 0).astype(jnp.float32)
        index_head_gains = lax.dynamic_slice_in_dim(index_gains, start, BLK, 0).astype(jnp.float32)
        inner = jnp.einsum("qjd,kd->qjk", indexer_query_rows, indexer_key_rows)
        live_heads = jnp.maximum(inner, 0.0)
        logits = jnp.einsum("qj,qjk->qk", index_head_gains, live_heads, precision=lax.Precision.HIGHEST)
        divergence, logit_gradient = kl_terms(mass_sum, logits, allowed)
        head_gains_gradient = jnp.einsum("qk,qjk->qj", logit_gradient, live_heads, precision=lax.Precision.HIGHEST)
        inner_gradient = jnp.where(inner > 0, logit_gradient[:, None, :] * index_head_gains[:, :, None], 0.0)
        rounded = lax.optimization_barrier(inner_gradient.astype(jnp.bfloat16)).astype(jnp.float32)
        query_grad = jnp.einsum("qjk,kd->qjd", rounded, indexer_key_rows).astype(jnp.bfloat16)
        key_grad = jnp.einsum("qjk,qjd->kd", rounded, indexer_query_rows)
        carry = carry.at[picked].add(key_grad[:picked_count * BLK].reshape(picked_count, BLK, IDIM))
        return carry, (divergence, query_grad, head_gains_gradient, key_grad[picked_count * BLK:])

    initial = jnp.zeros((PREFIX // BLK, BLK, IDIM), jnp.float32)
    cache_grad, stacked = lax.scan(step, initial, jnp.arange(QUERIES // BLK, dtype=jnp.int32))
    divergence, query_grad, head_gains_gradient, stretch_grad = stacked
    return (divergence.reshape(QUERIES), query_grad.reshape(QUERIES, IHEADS, IDIM),
            head_gains_gradient.reshape(QUERIES, IHEADS), cache_grad.reshape(PREFIX, IDIM),
            stretch_grad.reshape(QUERIES, IDIM))
```

```python
import functools

import jax
import jax.numpy as jnp
from jax import lax
from jax.experimental import pallas as pl
from jax.experimental.pallas import tpu as pltpu
from jax.sharding import PartitionSpec as P

MESH = pl.DeviceIdType.MESH
HEADS = 128
SCORE_SCALE = 192.0 ** (-0.5)
LOG2E = 1.4426950408889634
BLK = 64
PICKED = 7
QBLK = 4
NX = 4
NZ = 8
NP = 8
QROWS = BLK // NX
KDIM = 576
IDIM = 128
SPAN = 512


def z_place(offset):
    return jnp.where(offset == 0, 0, jnp.where(offset <= 4, 2 * offset - 1, 2 * (8 - offset)))


def place_offset(place):
    return jnp.where(place % 2 == 1, (place + 1) // 2, NZ - place // 2)


def gather_kernel(
    ids,
    cl,
    ci,
    sl,
    si,
    out_latent,
    out_index,
    out_want,
    *scratch,
):
    stock_l, stock_i = scratch[:NZ], scratch[NZ : 2 * NZ]
    send_l, send_i, recv_l, recv_i, key_l, key_i, want_v, want_s = scratch[2 * NZ : 2 * NZ + 8]
    local_sem, ids_send, ids_recv, z_send, z_recv, y_send, y_recv, x_send, x_recv = scratch[
        2 * NZ + 8 :
    ]
    seq = lax.axis_index("seq")
    h = lax.axis_index("head")
    z, me = seq // NP, seq % NP
    z_next, z_prev = ((z + 1) % NZ) * NP + me, ((z + NZ - 1) % NZ) * NP + me
    x_next, x_prev = (h + 1) % NX, (h + NX - 1) % NX

    loads = [
        pltpu.make_async_copy(cl.at[:, h], stock_l[0], local_sem.at[0]),
        pltpu.make_async_copy(ci.at[:, h], stock_i[0], local_sem.at[1]),
        pltpu.make_async_copy(sl, key_l.at[:, PICKED], local_sem.at[2]),
        pltpu.make_async_copy(si, key_i.at[:, PICKED], local_sem.at[3]),
    ]
    for load in loads:
        load.start()

    barrier = pltpu.get_barrier_semaphore()
    for target in ((z_next, h), (z_prev, h), (seq, x_next), (seq, x_prev)):
        pl.semaphore_signal(barrier, inc=1, device_id=target, device_id_type=MESH)

    def greet(i, _):
        pl.semaphore_signal(
            barrier, inc=1, device_id=(z * NP + (me + i) % NP, h), device_id_type=MESH
        )
        return 0

    lax.fori_loop(1, NP, greet, 0)

    lane = lax.broadcasted_iota(jnp.int32, (8, 128), 1)
    row = lax.broadcasted_iota(jnp.int32, (8, 128), 0)
    tile = jnp.full((8, 128), -1, jnp.int32)
    for r in range(QBLK):
        for j in range(PICKED):
            block = ids[r, j]
            owner = block >> 3
            spot = (owner & 7) * NZ + z_place(((owner >> 3) - z + NZ) & 7)
            value = jnp.where(row == 0, block & 7, r * 8 + j)
            tile = jnp.where(lane == spot, value, tile)
    want_v[me] = tile

    pl.semaphore_wait(barrier, 4 + NP - 1)

    def ids_copy(i):
        peer = (me + i) % NP
        return pltpu.make_async_remote_copy(
            src_ref=want_v.at[me],
            dst_ref=want_v.at[me],
            send_sem=ids_send.at[i],
            recv_sem=ids_recv.at[i],
            device_id=(z * NP + peer, h),
            device_id_type=MESH,
        )

    def ids_start(i, _):
        ids_copy(i).start()
        return 0

    lax.fori_loop(1, NP, ids_start, 0)

    def z_copies(step, way):
        if way == 0:
            src, dst = 2 * (step - 1), 2 * step if step < 4 else 7
            part, target = pl.ds(0, 4), z_next
        else:
            src, dst = max(2 * step - 3, 0), 2 * step - 1
            part, target = pl.ds(4, 4), z_prev
        if step < 4:
            part = pl.ds(0, 8)
        return [
            pltpu.make_async_remote_copy(
                src_ref=stock[src].at[part],
                dst_ref=stock[dst].at[part],
                send_sem=z_send.at[a, way, step],
                recv_sem=z_recv.at[a, way, step],
                device_id=(target, h),
                device_id_type=MESH,
            )
            for a, stock in enumerate((stock_l, stock_i))
        ]

    loads[0].wait()
    loads[1].wait()
    for way in range(2):
        for copy in z_copies(1, way):
            copy.start()

    def ids_wait(i, _):
        ids_copy(i).wait()
        return 0

    lax.fori_loop(1, NP, ids_wait, 0)
    to_scalar = pltpu.make_async_copy(want_v, want_s, local_sem.at[4])
    to_scalar.start()
    to_scalar.wait()

    def y_copies(i, step, first, count):
        peer = (me + i) % NP
        return [
            pltpu.make_async_remote_copy(
                src_ref=send.at[peer, pl.ds(first, count)],
                dst_ref=recv.at[me, pl.ds(first, count)],
                send_sem=y_send.at[a, step, i],
                recv_sem=y_recv.at[a, step, i],
                device_id=(z * NP + peer, h),
                device_id_type=MESH,
            )
            for a, (send, recv) in enumerate(((send_l, recv_l), (send_i, recv_i)))
        ]

    spans = ((0, 1), (1, 2), (3, 2), (5, 2), (7, 1))
    for step, (first, count) in enumerate(spans):
        if step:
            for way in range(2):
                for copy in z_copies(step, way):
                    copy.wait_recv()
            if step < 4:
                for way in range(2):
                    for copy in z_copies(step + 1, way):
                        copy.start()

        def stage(i, _, step=step, first=first, count=count):
            peer = (me + i) % NP
            for q in range(first, first + count):
                block = jnp.maximum(want_s[peer, 0, me * NZ + q], 0)
                send_l[peer, q] = stock_l[q][block]
                send_i[peer, q] = stock_i[q][block]
            for copy in y_copies(i, step, first, count):
                copy.start()
            return 0

        lax.fori_loop(1, NP, stage, 0)
        for q in range(first, first + count):
            block = jnp.maximum(want_s[me, 0, me * NZ + q], 0)
            recv_l[me, q] = stock_l[q][block]
            recv_i[me, q] = stock_i[q][block]

    for step, (first, count) in enumerate(spans):

        def y_wait(i, _, step=step, first=first, count=count):
            for copy in y_copies(i, step, first, count):
                copy.wait()
            return 0

        lax.fori_loop(1, NP, y_wait, 0)

    def x_copies(r, step, way):
        if step == 0:
            quarter, part = h, pl.ds(0, PICKED)
        elif way == 0:
            quarter, part = x_prev, pl.ds(0, 4)
        else:
            quarter, part = x_next, pl.ds(4, 3)
        return [
            pltpu.make_async_remote_copy(
                src_ref=key.at[r, part, quarter],
                dst_ref=key.at[r, part, quarter],
                send_sem=x_send.at[a, r, step, way],
                recv_sem=x_recv.at[a, r, step, way],
                device_id=(seq, x_prev if way else x_next),
                device_id_type=MESH,
            )
            for a, key in enumerate((key_l, key_i))
        ]

    for r in range(QBLK):
        for j in range(PICKED):
            owner = ids[r, j] >> 3
            place = z_place(((owner >> 3) - z + NZ) & 7)
            key_l[r, j, h] = recv_l[owner & 7, place]
            key_i[r, j, h] = recv_i[owner & 7, place]
        for way in range(2):
            for copy in x_copies(r, 0, way):
                copy.start()
    for r in range(QBLK):
        for way in range(2):
            for copy in x_copies(r, 0, way):
                copy.wait_recv()
        for way in range(2):
            for copy in x_copies(r, 1, way):
                copy.start()
    loads[2].wait()
    loads[3].wait()
    stores = []
    for r in range(QBLK):
        for way in range(2):
            for copy in x_copies(r, 1, way):
                copy.wait_recv()
        for a, (key, out) in enumerate(((key_l, out_latent), (key_i, out_index))):
            store = pltpu.make_async_copy(key.at[r], out.at[r], local_sem.at[5 + 2 * r + a])
            store.start()
            stores.append(store)
    store = pltpu.make_async_copy(want_v, out_want, local_sem.at[13])
    store.start()
    stores.append(store)
    for r in range(QBLK):
        for step in range(2):
            for way in range(2):
                for copy in x_copies(r, step, way):
                    copy.wait_send()
    for step in range(1, 5):
        for way in range(2):
            for copy in z_copies(step, way):
                copy.wait_send()
    for store in stores:
        store.wait()


def gather_keys(block_ids, cache_latent, cache_index, stretch_latent, stretch_index):
    bf16, sem = jnp.bfloat16, pltpu.SemaphoreType.DMA
    any_space = pl.BlockSpec(memory_space=pl.ANY)
    return pl.pallas_call(
        gather_kernel,
        out_shape=(
            jax.ShapeDtypeStruct((QBLK, 8, NX, QROWS, KDIM), bf16),
            jax.ShapeDtypeStruct((QBLK, 8, NX, QROWS, IDIM), bf16),
            jax.ShapeDtypeStruct((NP, 8, 128), jnp.int32),
        ),
        in_specs=[pl.BlockSpec(memory_space=pltpu.SMEM)] + [any_space] * 4,
        out_specs=(any_space,) * 3,
        scratch_shapes=[
            *[pltpu.VMEM((8, QROWS, KDIM), bf16)] * NZ,
            *[pltpu.VMEM((8, QROWS, IDIM), bf16)] * NZ,
            pltpu.VMEM((NP, NZ, QROWS, KDIM), bf16),
            pltpu.VMEM((NP, NZ, QROWS, IDIM), bf16),
            pltpu.VMEM((NP, NZ, QROWS, KDIM), bf16),
            pltpu.VMEM((NP, NZ, QROWS, IDIM), bf16),
            pltpu.VMEM((QBLK, 8, NX, QROWS, KDIM), bf16),
            pltpu.VMEM((QBLK, 8, NX, QROWS, IDIM), bf16),
            pltpu.VMEM((NP, 8, 128), jnp.int32),
            pltpu.SMEM((NP, 8, 128), jnp.int32),
            sem((14,)),
            sem((NP,)),
            sem((NP,)),
            sem((2, 2, 5)),
            sem((2, 2, 5)),
            sem((2, 5, NP)),
            sem((2, 5, NP)),
            sem((2, QBLK, 2, 2)),
            sem((2, QBLK, 2, 2)),
        ],
        compiler_params=pltpu.CompilerParams(
            collective_id=0, has_side_effects=True, vmem_limit_bytes=40 << 20
        ),
        name="gather_keys",
    )(
        block_ids,
        cache_latent.reshape(8, NX, QROWS, KDIM),
        cache_index.reshape(8, NX, QROWS, IDIM),
        stretch_latent.reshape(QBLK, NX, QROWS, KDIM),
        stretch_index.reshape(QBLK, NX, QROWS, IDIM),
    )


QUAD = 4
PART = 16


def forward_kernel(q, key_l, key_i, qi, gains, mass, logits, sums):
    step = pl.program_id(1)
    iheads = qi.shape[1]
    row = lax.broadcasted_iota(jnp.int32, (BLK, QUAD * BLK), 0)
    token = lax.broadcasted_iota(jnp.int32, (BLK, QUAD * BLK), 1) % BLK
    allowed = row <= token
    cut = PICKED * BLK
    scale = SCORE_SCALE * LOG2E
    for r in range(2):
        keys = key_l[r].reshape(SPAN, KDIM)
        queries = jnp.concatenate([q[i, :, r * BLK : (r + 1) * BLK] for i in range(QUAD)], axis=1)
        scores = jnp.dot(keys, queries, preferred_element_type=jnp.float32)
        old, own = scores[:cut], jnp.where(allowed, scores[cut:], -jnp.inf)
        top = jnp.maximum(jnp.max(old, axis=0, keepdims=True), jnp.max(own, axis=0, keepdims=True))
        e_old = jnp.exp2((old - top) * scale)
        e_own = jnp.exp2((own - top) * scale)
        total = jnp.sum(e_old, axis=0, keepdims=True) + jnp.sum(e_own, axis=0, keepdims=True)
        share = 1.0 / total

        @pl.when(step == 0)
        def _():
            sums[r, :cut] = e_old * share
            sums[r, cut:] = e_own * share

        @pl.when(step > 0)
        def _():
            sums[r, :cut] += e_old * share
            sums[r, cut:] += e_own * share

    ikeys = key_i[step // 4].reshape(SPAN, IDIM)
    tokens = pl.ds(pl.multiple_of(step * PART, PART), PART)
    iblock = qi[tokens].reshape(PART * iheads, IDIM)
    inner = lax.dot_general(
        iblock, ikeys, (((1,), (1,)), ((), ())), preferred_element_type=jnp.float32
    )
    gain = pltpu.roll(gains[...], 2 * BLK - step * PART, 1)
    rows = []
    for t in range(PART):
        live = jnp.maximum(inner[t * iheads : (t + 1) * iheads], 0.0)
        rows.append(jnp.sum(live * gain[:, t : t + 1], axis=0, keepdims=True))
    logits[tokens] = jnp.concatenate(rows, axis=0)

    @pl.when(step == pl.num_programs(1) - 1)
    def _():
        for r in range(2):
            pair = sums[r, :, : 2 * BLK] + sums[r, :, 2 * BLK :]
            mass[pl.ds(r * BLK, BLK)] = (pair[:, :BLK] + pair[:, BLK:]).T


def forward(query_latent, key_l, key_i, query_index, index_gains):
    rows, heads, _ = query_latent.shape
    iheads = query_index.shape[1]
    whole = lambda p, s: (p, 0, 0, 0, 0)
    return pl.pallas_call(
        forward_kernel,
        grid=(QBLK // 2, heads // QUAD),
        in_specs=[
            pl.BlockSpec((QUAD, KDIM, 2 * BLK), lambda p, s: (s, 0, p)),
            pl.BlockSpec((2, 8, NX, QROWS, KDIM), whole),
            pl.BlockSpec((2, 8, NX, QROWS, IDIM), whole),
            pl.BlockSpec((2 * BLK, iheads, IDIM), lambda p, s: (p, 0, 0)),
            pl.BlockSpec((iheads, 2 * BLK), lambda p, s: (0, p)),
        ],
        out_specs=[pl.BlockSpec((2 * BLK, SPAN), lambda p, s: (p, 0))] * 2,
        out_shape=[jax.ShapeDtypeStruct((rows, SPAN), jnp.float32)] * 2,
        scratch_shapes=[pltpu.VMEM((2, SPAN, QUAD * BLK), jnp.float32)],
        compiler_params=pltpu.CompilerParams(vmem_limit_bytes=48 << 20),
        name="forward",
    )(
        jnp.transpose(query_latent, (1, 2, 0)),
        key_l,
        key_i,
        query_index,
        index_gains.T,
    )


BCHUNK = 16


def backward_kernel(
    mass,
    logits,
    qi,
    gains,
    key_i,
    want,
    out_div,
    out_qgrad,
    out_ggrad,
    out_cache,
    out_own,
    mass_b,
    rs_m,
    rs_l,
    lg,
    div,
    kgrad,
    kquarter,
    kpart,
    krecv,
    slots,
    ret_s,
    ret_r,
    z_part,
    z_got,
    cache_g,
    own_g,
    out_sem,
    rs_send,
    rs_recv,
    lg_send,
    lg_recv,
    k_send,
    k_recv,
    y_send,
    y_recv,
    z_send,
    z_recv,
    f_send,
    f_recv,
    ggrad_t,
):
    seq = lax.axis_index("seq")
    h = lax.axis_index("head")
    z, me = seq // NP, seq % NP
    iheads = qi.shape[1]

    barrier = pltpu.get_barrier_semaphore()

    def greet_x(i, _):
        pl.semaphore_signal(
            barrier, inc=1, device_id=(seq, (h + i) % NX), device_id_type=MESH
        )
        return 0

    def greet_y(i, _):
        pl.semaphore_signal(
            barrier, inc=1, device_id=(z * NP + (me + i) % NP, h), device_id_type=MESH
        )
        return 0

    def greet_z(i, _):
        pl.semaphore_signal(
            barrier, inc=1, device_id=(((z + i) % NZ) * NP + me, h), device_id_type=MESH
        )
        return 0

    lax.fori_loop(1, NX, greet_x, 0)
    lax.fori_loop(1, NP, greet_y, 0)
    lax.fori_loop(1, NZ, greet_z, 0)
    for r in range(QBLK):
        mass_b[r] = mass[r].astype(jnp.bfloat16)
    pl.semaphore_wait(barrier, NX - 1 + NP - 1 + NZ - 1)

    def remote(src, dst, send, recv, target):
        return pltpu.make_async_remote_copy(
            src_ref=src,
            dst_ref=dst,
            send_sem=send,
            recv_sem=recv,
            device_id=target,
            device_id_type=MESH,
        )

    def each(count, copies, act):
        def body(i, _):
            for copy in copies(i):
                act(copy)
            return 0

        lax.fori_loop(1, count, body, 0)

    start = lambda copy: copy.start()
    wait = lambda copy: copy.wait()
    wait_recv = lambda copy: copy.wait_recv()
    wait_send = lambda copy: copy.wait_send()

    def rs_copies(i):
        peer = (h + i) % NX
        return [
            remote(mass_b.at[peer], rs_m.at[h], rs_send.at[0, i], rs_recv.at[0, i], (seq, peer)),
            remote(logits.at[peer], rs_l.at[h], rs_send.at[1, i], rs_recv.at[1, i], (seq, peer)),
        ]

    each(NX, rs_copies, start)
    each(NX, rs_copies, wait)
    mass_sum, logit = mass[h], logits[h]
    for i in range(1, NX):
        mass_sum = mass_sum + rs_m[(h + i) % NX].astype(jnp.float32)
        logit = logit + rs_l[(h + i) % NX]
    target = mass_sum * (1.0 / HEADS)
    column = lax.broadcasted_iota(jnp.int32, (BLK, SPAN), 1)
    token = lax.broadcasted_iota(jnp.int32, (BLK, SPAN), 0)
    allowed = column - PICKED * BLK <= token
    masked = jnp.where(allowed, logit, -jnp.inf)
    shifted = masked - jnp.max(masked, axis=1, keepdims=True)
    powers = jnp.exp(shifted)
    total = jnp.sum(powers, axis=1, keepdims=True)
    model = powers / total
    log_model = jnp.where(allowed, shifted - jnp.log(total), 0.0)
    safe = jnp.where(target > 0, target, 1.0)
    pointwise = jnp.where(allowed, target * (jnp.log(safe) - log_model), 0.0)
    divergence = jnp.sum(pointwise, axis=1, keepdims=True)
    lg[h] = jnp.where(allowed, model - target, 0.0).astype(jnp.bfloat16)
    diagonal = lax.broadcasted_iota(jnp.int32, (BLK, 128), 0) == lax.broadcasted_iota(
        jnp.int32, (BLK, 128), 1
    )
    in_lanes = jnp.sum(jnp.where(diagonal, divergence, 0.0), axis=0, keepdims=True)
    div[h] = jnp.broadcast_to(in_lanes, (8, 128))

    def lg_copies(i):
        peer = (h + i) % NX
        return [
            remote(lg.at[h], lg.at[h], lg_send.at[0, i], lg_recv.at[0, i], (seq, peer)),
            remote(div.at[h], div.at[h], lg_send.at[1, i], lg_recv.at[1, i], (seq, peer)),
        ]

    each(NX, lg_copies, start)

    def k_copy(i, r):
        peer = (h + i) % NX
        return remote(
            kpart.at[r, :, peer], krecv.at[h, r], k_send.at[i, r], k_recv.at[i, r], (seq, peer)
        )

    def backward(d, _):
        r = (h + NX - d) % NX

        @pl.when(d > 0)
        def _():
            for copy in lg_copies(d):
                copy.wait_recv()

        ikeys = key_i[r].reshape(SPAN, IDIM)
        kgrad[...] = jnp.zeros_like(kgrad)

        def part(c, _):
            first = pl.multiple_of(c * BCHUNK, BCHUNK)
            rows = pl.ds(r * BLK + first, BCHUNK)
            iblock = qi[rows].reshape(BCHUNK * iheads, IDIM)
            inner = lax.dot_general(
                iblock, ikeys, (((1,), (1,)), ((), ())), preferred_element_type=jnp.float32
            )
            slope = lg[r, pl.ds(first, BCHUNK)].astype(jnp.float32)
            start_lane = (r % 2) * BLK + first
            gain = pltpu.roll(gains[:, pl.ds(pl.multiple_of((r // 2) * 128, 128), 128)], 128 - start_lane, 1)
            lane = lax.broadcasted_iota(jnp.int32, (iheads, 128), 1)
            found = jnp.zeros((iheads, 128), jnp.float32)
            grads = []
            for t in range(BCHUNK):
                piece = inner[t * iheads : (t + 1) * iheads]
                push = slope[t : t + 1]
                gsum = jnp.sum(jnp.maximum(piece, 0.0) * push, axis=1, keepdims=True)
                found = jnp.where(lane == start_lane + t, gsum, found)
                grads.append(
                    jnp.where(piece > 0, push * gain[:, t : t + 1], 0.0).astype(jnp.bfloat16)
                )
            ggrad_t[r // 2] += found
            inner_grad = jnp.concatenate(grads, axis=0)
            qgrad = jnp.dot(inner_grad, ikeys, preferred_element_type=jnp.float32)
            out_qgrad[rows] = qgrad.astype(jnp.bfloat16).reshape(BCHUNK, iheads, IDIM)
            kgrad[...] += lax.dot_general(
                inner_grad, iblock, (((0,), (0,)), ((), ())), preferred_element_type=jnp.float32
            )
            return 0

        lax.fori_loop(0, BLK // BCHUNK, part, 0)
        for j in range(8):
            block = kgrad[pl.ds(j * BLK, BLK)].reshape(NX, QROWS, IDIM)
            kpart[r, j] = block.astype(jnp.bfloat16)
            kquarter[r, j] = kgrad[pl.ds(j * BLK + h * QROWS, QROWS)]

        def send(i, _):
            k_copy(i, r).start()
            return 0

        lax.fori_loop(1, NX, send, 0)
        return 0

    ggrad_t[...] = jnp.zeros_like(ggrad_t)
    lax.fori_loop(0, NX, backward, 0)
    out_ggrad[:, :128] = ggrad_t[0]
    out_ggrad[:, 128:] = ggrad_t[1]

    for r in range(QBLK):

        def k_wait(i, _, r=r):
            k_copy(i, r).wait()
            return 0

        lax.fori_loop(1, NX, k_wait, 0)
        total = kquarter[r]
        for i in range(1, NX):
            total = total + krecv[(h + i) % NX, r].astype(jnp.float32)
        own_g[r, h] = total[PICKED]
        slots[pl.ds(r * 8, 8)] = total.astype(jnp.bfloat16)

    def put_back(p, _):
        for q in range(NZ):
            slot = jnp.maximum(want[me, 1, p * NZ + q], 0)
            ret_s[p, q] = slots[slot]
        return 0

    lax.fori_loop(0, NP, put_back, 0)

    def y_copies(i):
        peer = (me + i) % NP
        return [
            remote(ret_s.at[peer], ret_r.at[me], y_send.at[i], y_recv.at[i], (z * NP + peer, h))
        ]

    each(NP, y_copies, start)

    def own_copies(i):
        peer = (h + i) % NX
        return [remote(own_g.at[:, h], own_g.at[:, h], f_send.at[0, i], f_recv.at[0, i], (seq, peer))]

    each(NX, own_copies, start)
    ret_r[me] = ret_s[me]
    each(NP, y_copies, wait)

    def add_up(q, _):
        sums = [jnp.zeros((QROWS, IDIM), jnp.float32) for _ in range(8)]
        for p in range(NP):
            block = want[p, 0, me * NZ + q]
            got = ret_r[p, q].astype(jnp.float32)
            for b in range(8):
                sums[b] = sums[b] + jnp.where(block == b, got, 0.0)
        for b in range(8):
            z_part[q, b] = sums[b].astype(jnp.bfloat16)
        return 0

    lax.fori_loop(0, NZ, add_up, 0)

    def z_copies(q):
        peer = ((z + place_offset(q)) % NZ) * NP + me
        return [remote(z_part.at[q], z_got.at[q], z_send.at[q], z_recv.at[q], (peer, h))]

    each(NZ, z_copies, start)
    each(NZ, z_copies, wait)
    cache_sum = z_part[0].astype(jnp.float32)
    for q in range(1, NZ):
        cache_sum = cache_sum + z_got[q].astype(jnp.float32)
    cache_g[:, h] = cache_sum

    def cache_copies(i):
        peer = (h + i) % NX
        return [
            remote(cache_g.at[:, h], cache_g.at[:, h], f_send.at[1, i], f_recv.at[1, i], (seq, peer))
        ]

    each(NX, cache_copies, start)
    each(NX, lg_copies, wait_send)
    out_div[...] = div[...]
    each(NX, own_copies, wait)
    own_store = pltpu.make_async_copy(own_g, out_own, out_sem.at[0])
    own_store.start()
    each(NX, cache_copies, wait)
    cache_store = pltpu.make_async_copy(cache_g, out_cache, out_sem.at[1])
    cache_store.start()
    own_store.wait()
    cache_store.wait()


def backward(mass, logits, query_index, index_gains, key_i, want):
    rows, iheads, _ = query_index.shape
    f32, bf16, sem = jnp.float32, jnp.bfloat16, pltpu.SemaphoreType.DMA
    vmem = pl.BlockSpec(memory_space=pltpu.VMEM)
    any_space = pl.BlockSpec(memory_space=pl.ANY)
    return pl.pallas_call(
        backward_kernel,
        out_shape=(
            jax.ShapeDtypeStruct((QBLK, 8, 128), f32),
            jax.ShapeDtypeStruct((rows, iheads, IDIM), bf16),
            jax.ShapeDtypeStruct((iheads, rows), f32),
            jax.ShapeDtypeStruct((8, NX, QROWS, IDIM), f32),
            jax.ShapeDtypeStruct((QBLK, NX, QROWS, IDIM), f32),
        ),
        in_specs=[vmem] * 5 + [pl.BlockSpec(memory_space=pltpu.SMEM)],
        out_specs=(vmem, vmem, vmem, any_space, any_space),
        scratch_shapes=[
            pltpu.VMEM((QBLK, BLK, SPAN), bf16),
            pltpu.VMEM((NX, BLK, SPAN), bf16),
            pltpu.VMEM((NX, BLK, SPAN), f32),
            pltpu.VMEM((QBLK, BLK, SPAN), bf16),
            pltpu.VMEM((QBLK, 8, 128), f32),
            pltpu.VMEM((SPAN, IDIM), f32),
            pltpu.VMEM((QBLK, 8, QROWS, IDIM), f32),
            pltpu.VMEM((QBLK, 8, NX, QROWS, IDIM), bf16),
            pltpu.VMEM((NX, QBLK, 8, QROWS, IDIM), bf16),
            pltpu.VMEM((QBLK * 8, QROWS, IDIM), bf16),
            pltpu.VMEM((NP, NZ, QROWS, IDIM), bf16),
            pltpu.VMEM((NP, NZ, QROWS, IDIM), bf16),
            pltpu.VMEM((NZ, 8, QROWS, IDIM), bf16),
            pltpu.VMEM((NZ, 8, QROWS, IDIM), bf16),
            pltpu.VMEM((8, NX, QROWS, IDIM), f32),
            pltpu.VMEM((QBLK, NX, QROWS, IDIM), f32),
            sem((2,)),
            sem((2, NX)),
            sem((2, NX)),
            sem((2, NX)),
            sem((2, NX)),
            sem((NX, QBLK)),
            sem((NX, QBLK)),
            sem((NP,)),
            sem((NP,)),
            sem((NZ,)),
            sem((NZ,)),
            sem((2, NX)),
            sem((2, NX)),
            pltpu.VMEM((2, iheads, 128), f32),
        ],
        compiler_params=pltpu.CompilerParams(
            collective_id=1, has_side_effects=True, vmem_limit_bytes=48 << 20
        ),
        name="backward",
    )(mass, logits, query_index, index_gains, key_i, want)


def per_device(
    query_latent,
    stretch_latent,
    cache_latent,
    query_index,
    stretch_index,
    cache_index,
    index_gains,
    block_ids,
):
    rows = query_latent.shape[0]
    key_l, key_i, want = gather_keys(
        block_ids, cache_latent, cache_index, stretch_latent, stretch_index
    )
    mass, logits = forward(query_latent, key_l, key_i, query_index, index_gains)
    divergence, qgrad, ggrad, cache_grad, own_grad = backward(
        mass.reshape(QBLK, BLK, SPAN),
        logits.reshape(QBLK, BLK, SPAN),
        query_index,
        index_gains.T,
        key_i,
        want,
    )
    return (
        divergence[:, 0, :BLK].reshape(rows),
        qgrad,
        ggrad.T,
        cache_grad.reshape(cache_index.shape),
        own_grad.reshape(stretch_index.shape),
    )


def solution(mesh):
    placed = (
        P("seq", "head", None),
        P("seq", None),
        P("seq", None),
        P("seq", "head", None),
        P("seq", None),
        P("seq", None),
        P("seq", "head"),
        P("seq", None),
    )
    return jax.shard_map(
        per_device,
        mesh=mesh,
        in_specs=placed,
        out_specs=(
            P("seq"),
            P("seq", "head", None),
            P("seq", "head"),
            P("seq", None),
            P("seq", None),
        ),
        check_vma=False,
    )
```

```python
import jax
import jax.numpy as jnp
from jax import lax
from jax.experimental import pallas as pl
from jax.experimental.pallas import tpu as pltpu
from jax.sharding import PartitionSpec as P

MESH = pl.DeviceIdType.MESH
HEADS = 128
SCORE_SCALE = 192.0 ** (-0.5)
LOG2E = 1.4426950408889634
BLK = 64
PICKED = 7
QBLK = 4
NX = 4
NZ = 8
NP = 8
QROWS = BLK // NX
KDIM = 576
IDIM = 128
SPAN = 512
HEAD_A = 256
WIDE_A, WIDE_B = IDIM + HEAD_A, KDIM - HEAD_A
OCT = 8
LOCAL_HEADS = 32
NOCT = LOCAL_HEADS // OCT
IHEADS = 16
PART = 16
ROWS = QBLK * BLK
CACHED = 512


def z_place(offset):
    return jnp.where(offset == 0, 0, jnp.where(offset <= 4, 2 * offset - 1, 2 * (8 - offset)))


def place_offset(place):
    return jnp.where(place % 2 == 1, (place + 1) // 2, NZ - place // 2)


def kernel(ids, cl, ci, sl, si, q, qi_h, gains_h, out_div, out_qgrad, out_ggrad, out_cache, out_own, *scratch):
    refs = list(scratch)
    take = lambda n: [refs.pop(0) for _ in range(n)]
    stock_a, stock_b = take(NZ), take(NZ)
    send_a, send_b, recv_a, recv_b, key_a, key_b, want_v, want_s = take(8)
    cl_v, sl_v, q_v, qr, qi, gains = take(6)
    sums, mass_o, mass_b, logits, rs_m, rs_l, lg, div = take(8)
    kgrad, kquarter, kpart, krecv, slots, ret_s, ret_r, z_part, z_got, cache_g, own_g = take(11)
    qgrad_v, ggrad_t = take(2)
    load_sem, q_sem, out_sem, ids_send, ids_recv, zs_send, zs_recv, ys_send, ys_recv = take(9)
    xs_send, xs_recv, rs_send, rs_recv, lg_send, lg_recv, k_send, k_recv = take(8)
    y_send, y_recv, z_send, z_recv, f_send, f_recv = take(6)

    seq = lax.axis_index("seq")
    h = lax.axis_index("head")
    z, me = seq // NP, seq % NP
    z_next, z_prev = ((z + 1) % NZ) * NP + me, ((z + NZ - 1) % NZ) * NP + me
    x_next, x_prev = (h + 1) % NX, (h + NX - 1) % NX
    quarter = pl.ds(pl.multiple_of(h * QROWS, QROWS), QROWS)

    def remote(src, dst, send, recv, target):
        return pltpu.make_async_remote_copy(
            src_ref=src,
            dst_ref=dst,
            send_sem=send,
            recv_sem=recv,
            device_id=target,
            device_id_type=MESH,
        )

    def each(count, copies, act):
        def body(i, _):
            for copy in copies(i):
                act(copy)
            return 0

        lax.fori_loop(1, count, body, 0)

    start = lambda copy: copy.start()
    wait = lambda copy: copy.wait()
    wait_recv = lambda copy: copy.wait_recv()
    wait_send = lambda copy: copy.wait_send()

    load_cl = pltpu.make_async_copy(cl, cl_v, load_sem.at[0])
    load_ci = pltpu.make_async_copy(ci.at[:, h], stock_a[0].at[:, :, pl.ds(0, IDIM)], load_sem.at[1])
    load_sl = pltpu.make_async_copy(sl, sl_v, load_sem.at[2])
    load_si = pltpu.make_async_copy(
        si, key_a.at[:, PICKED, :, :, pl.ds(0, IDIM)], load_sem.at[3]
    )
    load_qi = pltpu.make_async_copy(qi_h, qi, load_sem.at[4])
    load_gains = pltpu.make_async_copy(gains_h, gains, load_sem.at[5])
    load_q = [
        pltpu.make_async_copy(
            q.at[pl.ds(o * OCT, OCT)], q_v.at[pl.ds(o * OCT, OCT)], q_sem.at[o]
        )
        for o in range(NOCT)
    ]
    for load in [load_cl, load_ci, load_sl, load_si, *load_q, load_qi, load_gains]:
        load.start()

    barrier = pltpu.get_barrier_semaphore()

    def greet(count, target):
        def body(i, _):
            pl.semaphore_signal(barrier, inc=1, device_id=target(i), device_id_type=MESH)
            return 0

        lax.fori_loop(1, count, body, 0)

    greet(NZ, lambda i: (((z + i) % NZ) * NP + me, h))
    greet(NP, lambda i: (z * NP + (me + i) % NP, h))
    greet(NX, lambda i: (seq, (h + i) % NX))

    lane = lax.broadcasted_iota(jnp.int32, (8, 128), 1)
    row = lax.broadcasted_iota(jnp.int32, (8, 128), 0)
    tile = jnp.full((8, 128), -1, jnp.int32)
    for r in range(QBLK):
        for j in range(PICKED):
            block = ids[r, j]
            owner = block >> 3
            spot = (owner & 7) * NZ + z_place(((owner >> 3) - z + NZ) & 7)
            value = jnp.where(row == 0, block & 7, r * 8 + j)
            tile = jnp.where(lane == spot, value, tile)
    want_v[me] = tile

    load_cl.wait()
    for b in range(8):
        if b % 2 == 0:
            pair = cl_v[:, b * BLK : (b + 2) * BLK].T
        rows = pair[(b % 2) * BLK : (b % 2 + 1) * BLK].reshape(NX, QROWS, KDIM)
        mine = jnp.where(
            h == 0, rows[0], jnp.where(h == 1, rows[1], jnp.where(h == 2, rows[2], rows[3]))
        )
        stock_a[0][b, :, IDIM:] = mine[:, :HEAD_A]
        stock_b[0][b] = mine[:, HEAD_A:]
    load_ci.wait()
    pl.semaphore_wait(barrier, NX - 1 + NP - 1 + NZ - 1)

    def ids_copies(i):
        peer = (me + i) % NP
        return [
            remote(want_v.at[me], want_v.at[me], ids_send.at[i], ids_recv.at[i], (z * NP + peer, h))
        ]

    def zs_copy(a, step, way):
        stock = stock_b if a else stock_a
        if way == 0:
            src, dst = 2 * (step - 1), 2 * step if step < 4 else 7
            part, target = pl.ds(0, 4), z_next
        else:
            src, dst = max(2 * step - 3, 0), 2 * step - 1
            part, target = pl.ds(4, 4), z_prev
        if step < 4:
            part = pl.ds(0, 8)
        return remote(
            stock[src].at[part],
            stock[dst].at[part],
            zs_send.at[a, way, step],
            zs_recv.at[a, way, step],
            (target, h),
        )

    spans = ((0, 1), (1, 2), (3, 2), (5, 2), (7, 1))

    def ys_copy(a, step, i):
        first, count = spans[step]
        peer = (me + i) % NP
        send, recv = (send_b, recv_b) if a else (send_a, recv_a)
        return remote(
            send.at[peer, pl.ds(first, count)],
            recv.at[me, pl.ds(first, count)],
            ys_send.at[a, step, i],
            ys_recv.at[a, step, i],
            (z * NP + peer, h),
        )

    def stage(a, step):
        first, count = spans[step]
        stock, send, recv = (stock_b, send_b, recv_b) if a else (stock_a, send_a, recv_a)

        def body(i, _):
            peer = (me + i) % NP
            for p in range(first, first + count):
                block = jnp.maximum(want_s[peer, 0, me * NZ + p], 0)
                send[peer, p] = stock[p][block]
            ys_copy(a, step, i).start()
            return 0

        lax.fori_loop(1, NP, body, 0)
        for p in range(first, first + count):
            block = jnp.maximum(want_s[me, 0, me * NZ + p], 0)
            recv[me, p] = stock[p][block]

    def turn(a, step):
        for way in range(2):
            zs_copy(a, step, way).wait_recv()
            if step < 4:
                zs_copy(a, step + 1, way).start()

    def arrange(unit):
        p, o = unit % 2, unit // 2
        if p == 0:
            load_q[o].wait()
        for half in range(2):
            cut = slice(p * 128 + half * BLK, p * 128 + (half + 1) * BLK)
            qr[p * 2 + half, o] = jnp.concatenate(
                [q_v[o * OCT + i, :, cut] for i in range(OCT)], axis=1
            )

    for way in range(2):
        zs_copy(0, 1, way).start()
    for way in range(2):
        zs_copy(1, 1, way).start()
    each(NP, ids_copies, start)
    each(NP, ids_copies, wait)
    to_scalar = pltpu.make_async_copy(want_v, want_s, load_sem.at[6])
    to_scalar.start()
    to_scalar.wait()
    stage(0, 0)
    stage(1, 0)
    arrange(0)
    for step in range(1, 5):
        turn(0, step)
        stage(0, step)
        arrange(2 * step - 1)
        turn(1, step)
        stage(1, step)
        if step < 4:
            arrange(2 * step)

    load_sl.wait()
    for p in range(2):
        rows = sl_v[:, p * 128 : (p + 1) * 128].T
        for half in range(2):
            own = rows[half * BLK : (half + 1) * BLK].reshape(NX, QROWS, KDIM)
            key_a[2 * p + half, PICKED, :, :, IDIM:] = own[:, :, :HEAD_A]
            key_b[2 * p + half, PICKED] = own[:, :, HEAD_A:]
    load_si.wait()

    def gathered(a):
        for step in range(len(spans)):
            each(NP, lambda i: [ys_copy(a, step, i)], wait)
        key, recv = (key_b, recv_b) if a else (key_a, recv_a)
        for r in range(QBLK):
            for j in range(PICKED):
                owner = ids[r, j] >> 3
                place = z_place(((owner >> 3) - z + NZ) & 7)
                key[r, j, h] = recv[owner & 7, place]

    def xs_copy(a, r, step, way):
        if step == 0:
            rows, part = h, pl.ds(0, PICKED)
        elif way == 0:
            rows, part = x_prev, pl.ds(0, 4)
        else:
            rows, part = x_next, pl.ds(4, 3)
        spot = (key_b if a else key_a).at[r, part, rows]
        return remote(
            spot,
            spot,
            xs_send.at[a, r, step, way],
            xs_recv.at[a, r, step, way],
            (seq, x_prev if way else x_next),
        )

    def xs_start(a, r):
        for way in range(2):
            xs_copy(a, r, 0, way).start()

    def xs_turn(a, r):
        for way in range(2):
            xs_copy(a, r, 0, way).wait_recv()
        for way in range(2):
            xs_copy(a, r, 1, way).start()

    def xs_done(a, r):
        for way in range(2):
            xs_copy(a, r, 1, way).wait_recv()

    gathered(0)
    for r in range(QBLK):
        xs_start(0, r)
    gathered(1)
    for r in range(QBLK):
        xs_turn(0, r)
        xs_start(1, r)

    def rs_copies(a, r):
        src, dst = (mass_b, rs_m) if a else (logits, rs_l)
        return remote(src.at[r], dst.at[h], rs_send.at[a, r], rs_recv.at[a, h], (seq, r))

    def rs_start(a, r):
        @pl.when(h != r)
        def _():
            rs_copies(a, r).start()

    def ikeys_of(r):
        return key_a[r, :, :, :, :IDIM].reshape(SPAN, IDIM)

    def gain_of(r, first):
        half = gains[:, (r // 2) * 128 : (r // 2 + 1) * 128]
        return pltpu.roll(half, 128 - (r % 2) * BLK - first, 1)

    def make_logits(r):
        ikeys = ikeys_of(r)

        def body(c, _):
            first = pl.multiple_of(c * PART, PART)
            iblock = qi[pl.ds(r * BLK + first, PART)].reshape(PART * IHEADS, IDIM)
            inner = lax.dot_general(
                iblock, ikeys, (((1,), (1,)), ((), ())), preferred_element_type=jnp.float32
            )
            gain = gain_of(r, first)
            rows = []
            for t in range(PART):
                live = jnp.maximum(inner[t * IHEADS : (t + 1) * IHEADS], 0.0)
                rows.append(jnp.sum(live * gain[:, t : t + 1], axis=0, keepdims=True))
            logits[r, pl.ds(first, PART)] = jnp.concatenate(rows, axis=0)
            return 0

        lax.fori_loop(0, BLK // PART, body, 0)
        rs_start(0, r)

    def make_mass(r):
        keys = jnp.concatenate(
            [
                key_a[r, :, :, :, IDIM:].reshape(SPAN, HEAD_A),
                key_b[r].reshape(SPAN, WIDE_B),
            ],
            axis=1,
        )
        cut = PICKED * BLK
        scale = SCORE_SCALE * LOG2E
        own_row = lax.broadcasted_iota(jnp.int32, (BLK, OCT * BLK), 0)
        token = lax.broadcasted_iota(jnp.int32, (BLK, OCT * BLK), 1) % BLK
        allowed = own_row <= token
        sums[...] = jnp.zeros_like(sums)

        def body(o, _):
            scores = jnp.dot(keys, qr[r, o], preferred_element_type=jnp.float32)
            old, own = scores[:cut], jnp.where(allowed, scores[cut:], -jnp.inf)
            top = jnp.maximum(
                jnp.max(old, axis=0, keepdims=True), jnp.max(own, axis=0, keepdims=True)
            )
            e_old = jnp.exp2((old - top) * scale)
            e_own = jnp.exp2((own - top) * scale)
            total = jnp.sum(e_old, axis=0, keepdims=True) + jnp.sum(e_own, axis=0, keepdims=True)
            share = 1.0 / total
            for lo, hi, e in ((0, cut, e_old), (cut, SPAN, e_own)):
                part = e * share
                fold = part[:, :128]
                for i in range(1, OCT // 2):
                    fold = fold + part[:, i * 128 : (i + 1) * 128]
                sums[lo:hi] += fold
            return 0

        lax.fori_loop(0, NOCT, body, 0)
        mass = (sums[:, :BLK] + sums[:, BLK:]).T

        @pl.when(h == r)
        def _():
            mass_o[...] = mass

        mass_b[r] = mass.astype(jnp.bfloat16)
        rs_start(1, r)

    def lg_copies(r, i):
        peer = (h + i) % NX
        return [
            remote(lg.at[r], lg.at[r], lg_send.at[0, i], lg_recv.at[0, r], (seq, peer)),
            remote(div.at[r], div.at[r], lg_send.at[1, i], lg_recv.at[1, r], (seq, peer)),
        ]

    def divergence_of(r):
        for i in range(1, NX):
            peer = (h + i) % NX
            for a, (src, dst) in enumerate(((logits, rs_l), (mass_b, rs_m))):
                remote(
                    src.at[r], dst.at[peer], rs_send.at[a, r], rs_recv.at[a, peer], (seq, peer)
                ).wait_recv()
        mass_sum, logit = mass_o[...], logits[r]
        for i in range(1, NX):
            mass_sum = mass_sum + rs_m[(h + i) % NX].astype(jnp.float32)
            logit = logit + rs_l[(h + i) % NX]
        target = mass_sum * (1.0 / HEADS)
        column = lax.broadcasted_iota(jnp.int32, (BLK, SPAN), 1)
        token = lax.broadcasted_iota(jnp.int32, (BLK, SPAN), 0)
        allowed = column - PICKED * BLK <= token
        masked = jnp.where(allowed, logit, -jnp.inf)
        shifted = masked - jnp.max(masked, axis=1, keepdims=True)
        powers = jnp.exp(shifted)
        total = jnp.sum(powers, axis=1, keepdims=True)
        model = powers / total
        log_model = jnp.where(allowed, shifted - jnp.log(total), 0.0)
        safe = jnp.where(target > 0, target, 1.0)
        pointwise = jnp.where(allowed, target * (jnp.log(safe) - log_model), 0.0)
        divergence = jnp.sum(pointwise, axis=1, keepdims=True)
        lg[r] = jnp.where(allowed, model - target, 0.0).astype(jnp.bfloat16)
        each(NX, lambda i: lg_copies(r, i)[:1], start)
        diagonal = lax.broadcasted_iota(jnp.int32, (BLK, 128), 0) == lax.broadcasted_iota(
            jnp.int32, (BLK, 128), 1
        )
        in_lanes = jnp.sum(jnp.where(diagonal, divergence, 0.0), axis=0, keepdims=True)
        div[r] = jnp.broadcast_to(in_lanes, (8, 128))
        each(NX, lambda i: lg_copies(r, i)[1:], start)

    def k_copy(i, r):
        peer = (h + i) % NX
        return remote(
            kpart.at[r, :, peer], krecv.at[h, r], k_send.at[i, r], k_recv.at[i, r], (seq, peer)
        )

    def qgrad_copy(r):
        rows = pl.ds(r * BLK, BLK)
        return pltpu.make_async_copy(qgrad_v.at[rows], out_qgrad.at[rows], out_sem.at[r])

    def backward(r):
        @pl.when(h != r)
        def _():
            lg_copies(r, 1)[0].wait_recv()

        ikeys = ikeys_of(r)
        kgrad[...] = jnp.zeros_like(kgrad)
        ggrad_t[...] = jnp.zeros_like(ggrad_t)

        def body(c, _):
            first = pl.multiple_of(c * PART, PART)
            rows = pl.ds(r * BLK + first, PART)
            iblock = qi[rows].reshape(PART * IHEADS, IDIM)
            inner = lax.dot_general(
                iblock, ikeys, (((1,), (1,)), ((), ())), preferred_element_type=jnp.float32
            )
            slope = lg[r, pl.ds(first, PART)].astype(jnp.float32)
            gain = gain_of(r, first)
            lanes = lax.broadcasted_iota(jnp.int32, (IHEADS, 128), 1)
            found = jnp.zeros((IHEADS, 128), jnp.float32)
            grads = []
            for t in range(PART):
                piece = inner[t * IHEADS : (t + 1) * IHEADS]
                push = slope[t : t + 1]
                gsum = jnp.sum(jnp.maximum(piece, 0.0) * push, axis=1, keepdims=True)
                found = jnp.where(lanes == first + t, gsum, found)
                grads.append(
                    jnp.where(piece > 0, push * gain[:, t : t + 1], 0.0).astype(jnp.bfloat16)
                )
            ggrad_t[...] += found
            inner_grad = jnp.concatenate(grads, axis=0)
            qgrad = jnp.dot(inner_grad, ikeys, preferred_element_type=jnp.float32)
            qgrad_v[rows] = qgrad.astype(jnp.bfloat16).reshape(PART, IHEADS, IDIM)
            kgrad[...] += lax.dot_general(
                inner_grad, iblock, (((0,), (0,)), ((), ())), preferred_element_type=jnp.float32
            )
            return 0

        lax.fori_loop(0, BLK // PART, body, 0)
        for j in range(8):
            block = kgrad[pl.ds(j * BLK, BLK)].reshape(NX, QROWS, IDIM)
            kpart[r, j] = block.astype(jnp.bfloat16)
            kquarter[r, j] = kgrad[pl.ds(pl.multiple_of(j * BLK + h * QROWS, QROWS), QROWS)]
        each(NX, lambda i: [k_copy(i, r)], start)
        qgrad_copy(r).start()
        out_ggrad[:, r * BLK : (r + 1) * BLK] = ggrad_t[:, :BLK]

    def owner_step(r):
        @pl.when(h == r)
        def _():
            divergence_of(r)

    load_qi.wait()
    load_gains.wait()
    for r in range(QBLK):
        xs_done(0, r)
        make_logits(r)
        if r < QBLK - 1:
            xs_turn(1, r)
    for r in range(QBLK):
        xs_done(1, r)
        make_mass(r)
        if r == 0:
            xs_turn(1, QBLK - 1)
        if r >= 1:
            owner_step(r - 1)
        if r >= 2:
            backward(r - 2)
    owner_step(QBLK - 1)
    backward(QBLK - 2)
    backward(QBLK - 1)

    for r in range(QBLK):
        each(NX, lambda i: [k_copy(i, r)], wait)
        total = kquarter[r]
        for i in range(1, NX):
            total = total + krecv[(h + i) % NX, r].astype(jnp.float32)
        own_g[r, h] = total[PICKED]
        slots[pl.ds(r * 8, 8)] = total.astype(jnp.bfloat16)

    def put_back(p, _):
        for place in range(NZ):
            slot = jnp.maximum(want_s[me, 1, p * NZ + place], 0)
            ret_s[p, place] = slots[slot]
        return 0

    lax.fori_loop(0, NP, put_back, 0)

    def y_copies(i):
        peer = (me + i) % NP
        return [
            remote(ret_s.at[peer], ret_r.at[me], y_send.at[i], y_recv.at[i], (z * NP + peer, h))
        ]

    each(NP, y_copies, start)

    def own_copies(i):
        peer = (h + i) % NX
        return [remote(own_g.at[:, h], own_g.at[:, h], f_send.at[0, i], f_recv.at[0, i], (seq, peer))]

    each(NX, own_copies, start)
    ret_r[me] = ret_s[me]
    each(NP, y_copies, wait)

    def z_copies(place):
        peer = ((z + place_offset(place)) % NZ) * NP + me
        return [remote(z_part.at[place], z_got.at[place], z_send.at[place], z_recv.at[place], (peer, h))]

    def add_up(place, _):
        sums8 = [jnp.zeros((QROWS, IDIM), jnp.float32) for _ in range(8)]
        for p in range(NP):
            block = want_s[p, 0, me * NZ + place]
            got = ret_r[p, place].astype(jnp.float32)
            for b in range(8):
                sums8[b] = sums8[b] + jnp.where(block == b, got, 0.0)
        for b in range(8):
            z_part[place, b] = sums8[b].astype(jnp.bfloat16)

        @pl.when(place > 0)
        def _():
            for copy in z_copies(place):
                copy.start()

        return 0

    lax.fori_loop(0, NZ, add_up, 0)

    for step in range(1, 5):
        for way in range(2):
            for a in range(2):
                zs_copy(a, step, way).wait_send()
    for a in range(2):
        for r in range(QBLK):
            for step in range(2):
                for way in range(2):
                    xs_copy(a, r, step, way).wait_send()
    for r in range(QBLK):

        @pl.when(h != r)
        def _():
            rs_copies(0, r).wait_send()
            rs_copies(1, r).wait_send()
            lg_copies(r, 1)[1].wait_recv()

        @pl.when(h == r)
        def _():
            each(NX, lambda i: lg_copies(r, i), wait_send)

    out_div[...] = div[...]
    for r in range(QBLK):
        qgrad_copy(r).wait()

    each(NZ, z_copies, wait)
    cache_sum = z_part[0].astype(jnp.float32)
    for place in range(1, NZ):
        cache_sum = cache_sum + z_got[place].astype(jnp.float32)
    cache_g[:, h] = cache_sum

    def cache_copies(i):
        peer = (h + i) % NX
        return [
            remote(cache_g.at[:, h], cache_g.at[:, h], f_send.at[1, i], f_recv.at[1, i], (seq, peer))
        ]

    each(NX, cache_copies, start)
    each(NX, own_copies, wait)
    own_store = pltpu.make_async_copy(own_g, out_own, out_sem.at[4])
    own_store.start()
    each(NX, cache_copies, wait)
    cache_store = pltpu.make_async_copy(cache_g, out_cache, out_sem.at[5])
    cache_store.start()
    own_store.wait()
    cache_store.wait()


def per_device(
    query_latent,
    stretch_latent,
    cache_latent,
    query_index,
    stretch_index,
    cache_index,
    index_gains,
    block_ids,
):
    f32, bf16, sem, V = jnp.float32, jnp.bfloat16, pltpu.SemaphoreType.DMA, pltpu.VMEM
    vmem = pl.BlockSpec(memory_space=pltpu.VMEM)
    any_space = pl.BlockSpec(memory_space=pl.ANY)
    divergence, qgrad, ggrad, cache_grad, own_grad = pl.pallas_call(
        kernel,
        out_shape=(
            jax.ShapeDtypeStruct((QBLK, 8, 128), f32),
            jax.ShapeDtypeStruct((ROWS, IHEADS, IDIM), bf16),
            jax.ShapeDtypeStruct((IHEADS, ROWS), f32),
            jax.ShapeDtypeStruct((8, NX, QROWS, IDIM), f32),
            jax.ShapeDtypeStruct((QBLK, NX, QROWS, IDIM), f32),
        ),
        in_specs=[pl.BlockSpec(memory_space=pltpu.SMEM)] + [any_space] * 7,
        out_specs=(vmem, any_space, vmem, any_space, any_space),
        scratch_shapes=[
            *[V((8, QROWS, WIDE_A), bf16)] * NZ,
            *[V((8, QROWS, WIDE_B), bf16)] * NZ,
            V((NP, NZ, QROWS, WIDE_A), bf16),
            V((NP, NZ, QROWS, WIDE_B), bf16),
            V((NP, NZ, QROWS, WIDE_A), bf16),
            V((NP, NZ, QROWS, WIDE_B), bf16),
            V((QBLK, 8, NX, QROWS, WIDE_A), bf16),
            V((QBLK, 8, NX, QROWS, WIDE_B), bf16),
            V((NP, 8, 128), jnp.int32),
            pltpu.SMEM((NP, 8, 128), jnp.int32),
            V((KDIM, CACHED), bf16),
            V((KDIM, ROWS), bf16),
            V((LOCAL_HEADS, KDIM, ROWS), bf16),
            V((QBLK, NOCT, KDIM, OCT * BLK), bf16),
            V((ROWS, IHEADS, IDIM), bf16),
            V((IHEADS, ROWS), f32),
            V((SPAN, 128), f32),
            V((BLK, SPAN), f32),
            V((QBLK, BLK, SPAN), bf16),
            V((QBLK, BLK, SPAN), f32),
            V((NX, BLK, SPAN), bf16),
            V((NX, BLK, SPAN), f32),
            V((QBLK, BLK, SPAN), bf16),
            V((QBLK, 8, 128), f32),
            V((SPAN, IDIM), f32),
            V((QBLK, 8, QROWS, IDIM), f32),
            V((QBLK, 8, NX, QROWS, IDIM), bf16),
            V((NX, QBLK, 8, QROWS, IDIM), bf16),
            V((QBLK * 8, QROWS, IDIM), bf16),
            V((NP, NZ, QROWS, IDIM), bf16),
            V((NP, NZ, QROWS, IDIM), bf16),
            V((NZ, 8, QROWS, IDIM), bf16),
            V((NZ, 8, QROWS, IDIM), bf16),
            V((8, NX, QROWS, IDIM), f32),
            V((QBLK, NX, QROWS, IDIM), f32),
            V((ROWS, IHEADS, IDIM), bf16),
            V((IHEADS, 128), f32),
            sem((7,)),
            sem((NOCT,)),
            sem((6,)),
            sem((NP,)),
            sem((NP,)),
            sem((2, 2, 5)),
            sem((2, 2, 5)),
            sem((2, 5, NP)),
            sem((2, 5, NP)),
            sem((2, QBLK, 2, 2)),
            sem((2, QBLK, 2, 2)),
            sem((2, QBLK)),
            sem((2, NX)),
            sem((2, NX)),
            sem((2, QBLK)),
            sem((NX, QBLK)),
            sem((NX, QBLK)),
            sem((NP,)),
            sem((NP,)),
            sem((NZ,)),
            sem((NZ,)),
            sem((2, NX)),
            sem((2, NX)),
        ],
        compiler_params=pltpu.CompilerParams(
            collective_id=0, has_side_effects=True, vmem_limit_bytes=60 << 20
        ),
        name="indexer_kl",
    )(
        block_ids,
        cache_latent.T,
        cache_index.reshape(8, NX, QROWS, IDIM),
        stretch_latent.T,
        stretch_index.reshape(QBLK, NX, QROWS, IDIM),
        jnp.transpose(query_latent, (1, 2, 0)),
        query_index,
        index_gains.T,
    )
    return (
        divergence[:, 0, :BLK].reshape(ROWS),
        qgrad,
        ggrad.T,
        cache_grad.reshape(CACHED, IDIM),
        own_grad.reshape(ROWS, IDIM),
    )


def solution(mesh):
    placed = (
        P("seq", "head", None),
        P("seq", None),
        P("seq", None),
        P("seq", "head", None),
        P("seq", None),
        P("seq", None),
        P("seq", "head"),
        P("seq", None),
    )
    return jax.shard_map(
        per_device,
        mesh=mesh,
        in_specs=placed,
        out_specs=(
            P("seq"),
            P("seq", "head", None),
            P("seq", "head"),
            P("seq", None),
            P("seq", None),
        ),
        check_vma=False,
    )
```

```python
import jax
import jax.numpy as jnp
from jax import lax
from jax.experimental import pallas as pl
from jax.experimental.pallas import tpu as pltpu
from jax.sharding import PartitionSpec as P

MESH = pl.DeviceIdType.MESH
HEADS = 128
SCORE_SCALE = 192.0 ** (-0.5)
LOG2E = 1.4426950408889634
BLK = 64
LAG = 2
PICKED = 7
QBLK = 4
NX = 4
NZ = 8
NP = 8
QROWS = BLK // NX
KDIM = 576
IDIM = 128
SPAN = 512
HEAD_A = 256
WIDE_A, WIDE_B = IDIM + HEAD_A, KDIM - HEAD_A
OCT = 8
LOCAL_HEADS = 32
NOCT = LOCAL_HEADS // OCT
IHEADS = 16
PART = 16
ROWS = QBLK * BLK
CACHED = 512


def z_place(offset):
    return jnp.where(offset == 0, 0, jnp.where(offset <= 4, 2 * offset - 1, 2 * (8 - offset)))


def place_offset(place):
    return jnp.where(place % 2 == 1, (place + 1) // 2, NZ - place // 2)


def kernel(ids, cl, ci, sl, si, q, qi_h, gains_h, out_div, out_qgrad, out_ggrad, out_cache, out_own, *scratch):
    refs = list(scratch)
    take = lambda n: [refs.pop(0) for _ in range(n)]
    stock_a, stock_b = take(NZ), take(NZ)
    send_a, send_b, recv_a, recv_b, key_a, key_b, want_v, want_s = take(8)
    cl_v, sl_v, q_v, qr, qi, gains = take(6)
    sums, mass_o, mass_b, logits, rs_m, rs_l, lg, div = take(8)
    kgrad, kquarter, kpart, krecv, slots, ret_s, ret_r, z_part, z_got, cache_g, own_g = take(11)
    ggrad_t, qgrad_v, ggrad_v, div_v = take(4)
    load_sem, q_sem, out_sem, ids_send, ids_recv, zs_send, zs_recv, ys_send, ys_recv = take(9)
    xs_send, xs_recv, rs_send, rs_recv, lg_send, lg_recv, k_send, k_recv = take(8)
    y_send, y_recv, z_send, z_recv, f_send, f_recv = take(6)

    seq = lax.axis_index("seq")
    h = lax.axis_index("head")
    z, me = seq // NP, seq % NP
    z_next, z_prev = ((z + 1) % NZ) * NP + me, ((z + NZ - 1) % NZ) * NP + me
    x_next, x_prev = (h + 1) % NX, (h + NX - 1) % NX
    quarter = pl.ds(pl.multiple_of(h * QROWS, QROWS), QROWS)

    def remote(src, dst, send, recv, target):
        return pltpu.make_async_remote_copy(
            src_ref=src,
            dst_ref=dst,
            send_sem=send,
            recv_sem=recv,
            device_id=target,
            device_id_type=MESH,
        )

    def each(count, copies, act):
        def body(i, _):
            for copy in copies(i):
                act(copy)
            return 0

        lax.fori_loop(1, count, body, 0)

    start = lambda copy: copy.start()
    wait = lambda copy: copy.wait()
    wait_recv = lambda copy: copy.wait_recv()
    wait_send = lambda copy: copy.wait_send()

    load_cl = pltpu.make_async_copy(cl, cl_v, load_sem.at[0])
    load_ci = pltpu.make_async_copy(ci.at[:, h], stock_a[0].at[:, :, pl.ds(0, IDIM)], load_sem.at[1])
    load_sl = pltpu.make_async_copy(sl, sl_v, load_sem.at[2])
    load_si = pltpu.make_async_copy(
        si, key_a.at[:, PICKED, :, :, pl.ds(0, IDIM)], load_sem.at[3]
    )
    load_qi = pltpu.make_async_copy(qi_h, qi, load_sem.at[4])
    load_gains = pltpu.make_async_copy(gains_h, gains, load_sem.at[5])
    load_q = [
        pltpu.make_async_copy(
            q.at[pl.ds(o * OCT, OCT)], q_v.at[pl.ds(o * OCT, OCT)], q_sem.at[o]
        )
        for o in range(NOCT)
    ]
    for load in [load_cl, load_ci, load_sl, load_si, *load_q, load_qi, load_gains]:
        load.start()

    barrier = pltpu.get_barrier_semaphore()

    def greet(count, target):
        def body(i, _):
            pl.semaphore_signal(barrier, inc=1, device_id=target(i), device_id_type=MESH)
            return 0

        lax.fori_loop(1, count, body, 0)

    greet(NZ, lambda i: (((z + i) % NZ) * NP + me, h))
    greet(NP, lambda i: (z * NP + (me + i) % NP, h))
    greet(NX, lambda i: (seq, (h + i) % NX))

    lane = lax.broadcasted_iota(jnp.int32, (8, 128), 1)
    row = lax.broadcasted_iota(jnp.int32, (8, 128), 0)
    tile = jnp.full((8, 128), -1, jnp.int32)
    for r in range(QBLK):
        for j in range(PICKED):
            block = ids[r, j]
            owner = block >> 3
            spot = (owner & 7) * NZ + z_place(((owner >> 3) - z + NZ) & 7)
            value = jnp.where(row == 0, block & 7, r * 8 + j)
            tile = jnp.where(lane == spot, value, tile)
    want_v[me] = tile

    load_cl.wait()
    for b in range(8):
        if b % 2 == 0:
            pair = cl_v[:, b * BLK : (b + 2) * BLK].T
        rows = pair[(b % 2) * BLK : (b % 2 + 1) * BLK].reshape(NX, QROWS, KDIM)
        mine = jnp.where(
            h == 0, rows[0], jnp.where(h == 1, rows[1], jnp.where(h == 2, rows[2], rows[3]))
        )
        stock_a[0][b, :, IDIM:] = mine[:, :HEAD_A]
        stock_b[0][b] = mine[:, HEAD_A:]
    load_ci.wait()
    pl.semaphore_wait(barrier, NX - 1 + NP - 1 + NZ - 1)

    def ids_copies(i):
        peer = (me + i) % NP
        return [
            remote(want_v.at[me], want_v.at[me], ids_send.at[i], ids_recv.at[i], (z * NP + peer, h))
        ]

    def zs_copy(a, step, way):
        stock = stock_b if a else stock_a
        if way == 0:
            src, dst = 2 * (step - 1), 2 * step if step < 4 else 7
            part, target = pl.ds(0, 4), z_next
        else:
            src, dst = max(2 * step - 3, 0), 2 * step - 1
            part, target = pl.ds(4, 4), z_prev
        if step < 4:
            part = pl.ds(0, 8)
        return remote(
            stock[src].at[part],
            stock[dst].at[part],
            zs_send.at[a, way, step],
            zs_recv.at[a, way, step],
            (target, h),
        )

    spans = ((0, 1), (1, 2), (3, 2), (5, 2), (7, 1))

    def ys_copy(a, step, i):
        first, count = spans[step]
        peer = (me + i) % NP
        send, recv = (send_b, recv_b) if a else (send_a, recv_a)
        return remote(
            send.at[peer, pl.ds(first, count)],
            recv.at[me, pl.ds(first, count)],
            ys_send.at[a, step, i],
            ys_recv.at[a, step, i],
            (z * NP + peer, h),
        )

    def stage(a, step):
        first, count = spans[step]
        stock, send, recv = (stock_b, send_b, recv_b) if a else (stock_a, send_a, recv_a)

        def body(i, _):
            peer = (me + i) % NP
            for p in range(first, first + count):
                block = jnp.maximum(want_s[peer, 0, me * NZ + p], 0)
                send[peer, p] = stock[p][block]
            ys_copy(a, step, i).start()
            return 0

        lax.fori_loop(1, NP, body, 0)
        for p in range(first, first + count):
            block = jnp.maximum(want_s[me, 0, me * NZ + p], 0)
            recv[me, p] = stock[p][block]

    def turn(a, step):
        for way in range(2):
            zs_copy(a, step, way).wait_recv()
            if step < 4:
                zs_copy(a, step + 1, way).start()

    def arrange(unit):
        p, o = unit % 2, unit // 2
        if p == 0:
            load_q[o].wait()
        for half in range(2):
            cut = slice(p * 128 + half * BLK, p * 128 + (half + 1) * BLK)
            qr[p * 2 + half, o] = jnp.concatenate(
                [q_v[o * OCT + i, :, cut] for i in range(OCT)], axis=1
            )

    def gathered(a):
        for step in range(len(spans)):
            each(NP, lambda i: [ys_copy(a, step, i)], wait)
        key, recv = (key_b, recv_b) if a else (key_a, recv_a)
        for r in range(QBLK):
            for j in range(PICKED):
                owner = ids[r, j] >> 3
                place = z_place(((owner >> 3) - z + NZ) & 7)
                key[r, j, h] = recv[owner & 7, place]

    def xs_copy(a, r, step, way):
        if step == 0:
            rows, part = h, pl.ds(0, PICKED)
        elif way == 0:
            rows, part = x_prev, pl.ds(0, 3 + r % 2)
        else:
            rows, part = x_next, pl.ds(3 + r % 2, 4 - r % 2)
        spot = (key_b if a else key_a).at[r, part, rows]
        return remote(
            spot,
            spot,
            xs_send.at[a, r, step, way],
            xs_recv.at[a, r, step, way],
            (seq, x_prev if way else x_next),
        )

    def xs_start(a, r):
        for way in range(2):
            xs_copy(a, r, 0, way).start()

    def xs_turn(a, r):
        for way in range(2):
            xs_copy(a, r, 0, way).wait_recv()
        for way in range(2):
            xs_copy(a, r, 1, way).start()

    def xs_done(a, r):
        for way in range(2):
            xs_copy(a, r, 1, way).wait_recv()

    def z_start(a):
        for way in range(2):
            zs_copy(a, 1, way).start()

    z_start(0)
    each(NP, ids_copies, start)
    each(NP, ids_copies, wait)
    to_scalar = pltpu.make_async_copy(want_v, want_s, load_sem.at[6])
    to_scalar.start()
    to_scalar.wait()
    stage(0, 0)
    arrange(0)
    for step in range(1, 5 + LAG):
        if step <= 4:
            turn(0, step)
        if step == LAG:
            z_start(1)
            stage(1, 0)
        if step <= 4:
            stage(0, step)
            arrange(step)
            if step == 4:
                gathered(0)
                for r in range(QBLK):
                    xs_start(0, r)
        if step > LAG:
            turn(1, step - LAG)
            stage(1, step - LAG)
            if step > 4:
                xs_turn(0, step - 5)
    for unit in range(5, 8):
        arrange(unit)
    load_sl.wait()
    for p in range(2):
        rows = sl_v[:, p * 128 : (p + 1) * 128].T
        for half in range(2):
            own = rows[half * BLK : (half + 1) * BLK].reshape(NX, QROWS, KDIM)
            key_a[2 * p + half, PICKED, :, :, IDIM:] = own[:, :, :HEAD_A]
            key_b[2 * p + half, PICKED] = own[:, :, HEAD_A:]
    load_si.wait()
    gathered(1)
    xs_start(1, 0)
    for r in range(LAG, QBLK):
        xs_turn(0, r)
        xs_start(1, r - LAG + 1)

    def rs_copies(r, i):
        peer = (h + i) % NX
        theirs = pl.ds(pl.multiple_of(peer * QROWS, QROWS), QROWS)
        return [
            remote(
                src.at[r, theirs], dst.at[r, h], rs_send.at[a, r, i], rs_recv.at[a, r, i], (seq, peer)
            )
            for a, (src, dst) in enumerate(((logits, rs_l), (mass_b, rs_m)))
        ]

    def ikeys_of(r):
        return key_a[r, :, :, :, :IDIM].reshape(SPAN, IDIM)

    def gain_of(r, first):
        half = gains[:, (r // 2) * 128 : (r // 2 + 1) * 128]
        return pltpu.roll(half, 128 - (r % 2) * BLK - first, 1)

    def make_logits(r):
        ikeys = ikeys_of(r)

        def body(c, _):
            first = pl.multiple_of(c * PART, PART)
            iblock = qi[pl.ds(r * BLK + first, PART)].reshape(PART * IHEADS, IDIM)
            inner = lax.dot_general(
                iblock, ikeys, (((1,), (1,)), ((), ())), preferred_element_type=jnp.float32
            )
            gain = gain_of(r, first)
            rows = []
            for t in range(PART):
                live = jnp.maximum(inner[t * IHEADS : (t + 1) * IHEADS], 0.0)
                rows.append(jnp.sum(live * gain[:, t : t + 1], axis=0, keepdims=True))
            logits[r, pl.ds(first, PART)] = jnp.concatenate(rows, axis=0)
            return 0

        lax.fori_loop(0, BLK // PART, body, 0)

    def make_mass(r):
        keys = jnp.concatenate(
            [
                key_a[r, :, :, :, IDIM:].reshape(SPAN, HEAD_A),
                key_b[r].reshape(SPAN, WIDE_B),
            ],
            axis=1,
        )
        cut = PICKED * BLK
        scale = SCORE_SCALE * LOG2E
        own_row = lax.broadcasted_iota(jnp.int32, (BLK, OCT * BLK), 0)
        token = lax.broadcasted_iota(jnp.int32, (BLK, OCT * BLK), 1) % BLK
        allowed = own_row <= token
        sums[...] = jnp.zeros_like(sums)

        def body(o, _):
            scores = jnp.dot(keys, qr[r, o], preferred_element_type=jnp.float32)
            old, own = scores[:cut], jnp.where(allowed, scores[cut:], -jnp.inf)
            top = jnp.maximum(
                jnp.max(old, axis=0, keepdims=True), jnp.max(own, axis=0, keepdims=True)
            )
            e_old = jnp.exp2((old - top) * scale)
            e_own = jnp.exp2((own - top) * scale)
            total = jnp.sum(e_old, axis=0, keepdims=True) + jnp.sum(e_own, axis=0, keepdims=True)
            share = 1.0 / total
            for lo, hi, e in ((0, cut, e_old), (cut, SPAN, e_own)):
                part = e * share
                fold = part[:, :128]
                for i in range(1, OCT // 2):
                    fold = fold + part[:, i * 128 : (i + 1) * 128]
                sums[lo:hi] += fold
            return 0

        lax.fori_loop(0, NOCT, body, 0)
        mass = (sums[:, :BLK] + sums[:, BLK:]).T

        mass_o[r] = mass
        mass_b[r] = mass.astype(jnp.bfloat16)
        each(NX, lambda i: rs_copies(r, i), start)

    def lg_copies(r, i):
        peer = (h + i) % NX
        return [remote(lg.at[r, quarter], lg.at[r, quarter], lg_send.at[r, i], lg_recv.at[r, i], (seq, peer))]

    def div_copies(i):
        peer = (h + i) % NX
        return [remote(div.at[h], div.at[h], lg_send.at[QBLK, i], lg_recv.at[QBLK, i], (seq, peer))]

    def divergence_of(r):
        each(NX, lambda i: rs_copies(r, i), wait)
        mass_sum, logit = mass_o[r, quarter], logits[r, quarter]
        for i in range(1, NX):
            mass_sum = mass_sum + rs_m[r, (h + i) % NX].astype(jnp.float32)
            logit = logit + rs_l[r, (h + i) % NX]
        target = mass_sum * (1.0 / HEADS)
        column = lax.broadcasted_iota(jnp.int32, (QROWS, SPAN), 1)
        token = lax.broadcasted_iota(jnp.int32, (QROWS, SPAN), 0) + h * QROWS
        allowed = column - PICKED * BLK <= token
        masked = jnp.where(allowed, logit, -jnp.inf)
        shifted = masked - jnp.max(masked, axis=1, keepdims=True)
        powers = jnp.exp(shifted)
        total = jnp.sum(powers, axis=1, keepdims=True)
        model = powers / total
        lg[r, quarter] = jnp.where(allowed, model - target, 0.0).astype(jnp.bfloat16)
        each(NX, lambda i: lg_copies(r, i), start)
        log_model = jnp.where(allowed, shifted - jnp.log(total), 0.0)
        safe = jnp.where(target > 0, target, 1.0)
        pointwise = jnp.where(allowed, target * (jnp.log(safe) - log_model), 0.0)
        divergence = jnp.sum(pointwise, axis=1, keepdims=True)
        spot = lax.broadcasted_iota(jnp.int32, (QROWS, 128), 1) == h * QROWS + (
            lax.broadcasted_iota(jnp.int32, (QROWS, 128), 0)
        )
        in_lanes = jnp.sum(jnp.where(spot, divergence, 0.0), axis=0, keepdims=True)
        return jnp.where(lax.broadcasted_iota(jnp.int32, (8, 128), 0) == r, in_lanes, 0.0)

    def k_copy(i, r):
        peer = (h + i) % NX
        return remote(
            kpart.at[r, :, peer], krecv.at[h, r], k_send.at[i, r], k_recv.at[i, r], (seq, peer)
        )

    def qgrad_copy(r):
        rows = pl.ds(r * BLK, BLK)
        return pltpu.make_async_copy(qgrad_v.at[rows], out_qgrad.at[rows], out_sem.at[r])

    stores = [
        pltpu.make_async_copy(src, dst, out_sem.at[QBLK + n])
        for n, (src, dst) in enumerate(
            ((ggrad_v, out_ggrad), (div_v, out_div), (own_g, out_own), (cache_g, out_cache))
        )
    ]

    def backward(r):
        each(NX, lambda i: lg_copies(r, i), wait)
        ikeys = ikeys_of(r)
        kgrad[...] = jnp.zeros_like(kgrad)
        ggrad_t[...] = jnp.zeros_like(ggrad_t)

        def body(c, _):
            first = pl.multiple_of(c * PART, PART)
            rows = pl.ds(r * BLK + first, PART)
            iblock = qi[rows].reshape(PART * IHEADS, IDIM)
            inner = lax.dot_general(
                iblock, ikeys, (((1,), (1,)), ((), ())), preferred_element_type=jnp.float32
            )
            slope = lg[r, pl.ds(first, PART)].astype(jnp.float32)
            gain = gain_of(r, first)
            lanes = lax.broadcasted_iota(jnp.int32, (IHEADS, 128), 1)
            found = jnp.zeros((IHEADS, 128), jnp.float32)
            grads = []
            for t in range(PART):
                piece = inner[t * IHEADS : (t + 1) * IHEADS]
                push = slope[t : t + 1]
                gsum = jnp.sum(jnp.maximum(piece, 0.0) * push, axis=1, keepdims=True)
                found = jnp.where(lanes == first + t, gsum, found)
                grads.append(
                    jnp.where(piece > 0, push * gain[:, t : t + 1], 0.0).astype(jnp.bfloat16)
                )
            ggrad_t[...] += found
            inner_grad = jnp.concatenate(grads, axis=0)
            qgrad = jnp.dot(inner_grad, ikeys, preferred_element_type=jnp.float32)
            qgrad_v[rows] = qgrad.astype(jnp.bfloat16).reshape(PART, IHEADS, IDIM)
            kgrad[...] += lax.dot_general(
                inner_grad, iblock, (((0,), (0,)), ((), ())), preferred_element_type=jnp.float32
            )
            return 0

        lax.fori_loop(0, BLK // PART, body, 0)
        for j in range(8):
            block = kgrad[pl.ds(j * BLK, BLK)].reshape(NX, QROWS, IDIM)
            kpart[r, j] = block.astype(jnp.bfloat16)
            kquarter[r, j] = kgrad[pl.ds(pl.multiple_of(j * BLK + h * QROWS, QROWS), QROWS)]
        each(NX, lambda i: [k_copy(i, r)], start)
        qgrad_copy(r).start()
        ggrad_v[:, r * BLK : (r + 1) * BLK] = ggrad_t[:, :BLK]

    load_qi.wait()
    load_gains.wait()
    for r in range(QBLK):
        xs_done(0, r)
        make_logits(r)
        if r < QBLK - 1:
            xs_turn(1, r)
            if r + QBLK - LAG + 1 < QBLK:
                xs_start(1, r + QBLK - LAG + 1)
    tiles = []
    for r in range(QBLK):
        xs_done(1, r)
        make_mass(r)
        if r == 0:
            xs_turn(1, QBLK - 1)
        if r >= 1:
            tiles.append(divergence_of(r - 1))
        if r >= 2:
            backward(r - 2)
    tiles.append(divergence_of(QBLK - 1))
    div[h] = sum(tiles[1:], tiles[0])
    each(NX, div_copies, start)
    backward(QBLK - 2)
    backward(QBLK - 1)

    for r in range(QBLK):
        each(NX, lambda i: [k_copy(i, r)], wait)
        total = kquarter[r]
        for i in range(1, NX):
            total = total + krecv[(h + i) % NX, r].astype(jnp.float32)
        own_g[r, h] = total[PICKED]
        slots[pl.ds(r * 8, 8)] = total.astype(jnp.bfloat16)

    stores[0].start()

    def put_back(p, _):
        for place in range(NZ):
            slot = jnp.maximum(want_s[me, 1, p * NZ + place], 0)
            ret_s[p, place] = slots[slot]
        return 0

    lax.fori_loop(0, NP, put_back, 0)

    groups = ((5, 3), (3, 2), (0, 3))

    def y_copies(g, i):
        peer = (me + i) % NP
        places = pl.ds(groups[g][0], groups[g][1])
        return [
            remote(
                ret_s.at[peer, places],
                ret_r.at[me, places],
                y_send.at[g, i],
                y_recv.at[g, i],
                (z * NP + peer, h),
            )
        ]

    for g in range(3):
        each(NP, lambda i: y_copies(g, i), start)

    def own_copies(i):
        peer = (h + i) % NX
        return [remote(own_g.at[:, h], own_g.at[:, h], f_send.at[0, i], f_recv.at[0, i], (seq, peer))]

    each(NX, own_copies, start)
    ret_r[me] = ret_s[me]

    def z_copies(place):
        peer = ((z + place_offset(place)) % NZ) * NP + me
        return [remote(z_part.at[place], z_got.at[place], z_send.at[place], z_recv.at[place], (peer, h))]

    def add_up(place, _):
        sums8 = [jnp.zeros((QROWS, IDIM), jnp.float32) for _ in range(8)]
        for p in range(NP):
            block = want_s[p, 0, me * NZ + place]
            got = ret_r[p, place].astype(jnp.float32)
            for b in range(8):
                sums8[b] = sums8[b] + jnp.where(block == b, got, 0.0)
        for b in range(8):
            z_part[place, b] = sums8[b].astype(jnp.bfloat16)

        @pl.when(place > 0)
        def _():
            for copy in z_copies(place):
                copy.start()

        return 0

    for g, (first, count) in enumerate(groups):
        each(NP, lambda i: y_copies(g, i), wait)
        lax.fori_loop(0, count, lambda i, _: add_up(first + count - 1 - i, 0), 0)

    for step in range(1, 5):
        for way in range(2):
            for a in range(2):
                zs_copy(a, step, way).wait_send()
    for a in range(2):
        for r in range(QBLK):
            for step in range(2):
                for way in range(2):
                    xs_copy(a, r, step, way).wait_send()
    each(NX, div_copies, wait)
    spread = div[0] + div[1] + div[2] + div[3]
    for p in range(2):
        div_v[p : p + 1] = jnp.concatenate(
            [spread[2 * p : 2 * p + 1, :BLK], spread[2 * p + 1 : 2 * p + 2, :BLK]], axis=1
        )
    stores[1].start()
    each(NX, own_copies, wait)
    stores[2].start()
    each(NZ, z_copies, wait)
    cache_sum = z_part[0].astype(jnp.float32)
    for place in range(1, NZ):
        cache_sum = cache_sum + z_got[place].astype(jnp.float32)
    cache_g[:, h] = cache_sum

    def cache_copies(i):
        peer = (h + i) % NX
        return [
            remote(cache_g.at[:, h], cache_g.at[:, h], f_send.at[1, i], f_recv.at[1, i], (seq, peer))
        ]

    each(NX, cache_copies, start)
    each(NX, cache_copies, wait)
    stores[3].start()
    for r in range(QBLK):
        qgrad_copy(r).wait()
    for store in stores:
        store.wait()


def emit_kernel(*refs):
    ins, outs, held, sems = refs[:5], refs[5:10], refs[10:15], refs[15]
    order = (1, 3, 4, 2, 0)
    loads = [pltpu.make_async_copy(ins[n], held[n], sems.at[0, n]) for n in range(5)]
    stores = [pltpu.make_async_copy(held[n], outs[n], sems.at[1, n]) for n in range(5)]
    for n in order:
        loads[n].start()
    for n in order:
        loads[n].wait()
        stores[n].start()
    for n in order:
        stores[n].wait()


def per_device(
    query_latent,
    stretch_latent,
    cache_latent,
    query_index,
    stretch_index,
    cache_index,
    index_gains,
    block_ids,
):
    f32, bf16, sem, V = jnp.float32, jnp.bfloat16, pltpu.SemaphoreType.DMA, pltpu.VMEM
    any_space = pl.BlockSpec(memory_space=pltpu.HBM)
    shapes = (
        jax.ShapeDtypeStruct((2, 128), f32),
        jax.ShapeDtypeStruct((ROWS, IHEADS, IDIM), bf16),
        jax.ShapeDtypeStruct((IHEADS, ROWS), f32),
        jax.ShapeDtypeStruct((8, NX, QROWS, IDIM), f32),
        jax.ShapeDtypeStruct((QBLK, NX, QROWS, IDIM), f32),
    )
    results = pl.pallas_call(
        kernel,
        out_shape=shapes,
        in_specs=[pl.BlockSpec(memory_space=pltpu.SMEM)] + [any_space] * 7,
        out_specs=(any_space,) * 5,
        scratch_shapes=[
            *[V((8, QROWS, WIDE_A), bf16)] * NZ,
            *[V((8, QROWS, WIDE_B), bf16)] * NZ,
            V((NP, NZ, QROWS, WIDE_A), bf16),
            V((NP, NZ, QROWS, WIDE_B), bf16),
            V((NP, NZ, QROWS, WIDE_A), bf16),
            V((NP, NZ, QROWS, WIDE_B), bf16),
            V((QBLK, 8, NX, QROWS, WIDE_A), bf16),
            V((QBLK, 8, NX, QROWS, WIDE_B), bf16),
            V((NP, 8, 128), jnp.int32),
            pltpu.SMEM((NP, 8, 128), jnp.int32),
            V((KDIM, CACHED), bf16),
            V((KDIM, ROWS), bf16),
            V((LOCAL_HEADS, KDIM, ROWS), bf16),
            V((QBLK, NOCT, KDIM, OCT * BLK), bf16),
            V((ROWS, IHEADS, IDIM), bf16),
            V((IHEADS, ROWS), f32),
            V((SPAN, 128), f32),
            V((QBLK, BLK, SPAN), f32),
            V((QBLK, BLK, SPAN), bf16),
            V((QBLK, BLK, SPAN), f32),
            V((QBLK, NX, QROWS, SPAN), bf16),
            V((QBLK, NX, QROWS, SPAN), f32),
            V((QBLK, BLK, SPAN), bf16),
            V((QBLK, 8, 128), f32),
            V((SPAN, IDIM), f32),
            V((QBLK, 8, QROWS, IDIM), f32),
            V((QBLK, 8, NX, QROWS, IDIM), bf16),
            V((NX, QBLK, 8, QROWS, IDIM), bf16),
            V((QBLK * 8, QROWS, IDIM), bf16),
            V((NP, NZ, QROWS, IDIM), bf16),
            V((NP, NZ, QROWS, IDIM), bf16),
            V((NZ, 8, QROWS, IDIM), bf16),
            V((NZ, 8, QROWS, IDIM), bf16),
            V((8, NX, QROWS, IDIM), f32),
            V((QBLK, NX, QROWS, IDIM), f32),
            V((IHEADS, 128), f32),
            V((ROWS, IHEADS, IDIM), bf16),
            V((IHEADS, ROWS), f32),
            V((2, 128), f32),
            sem((7,)),
            sem((NOCT,)),
            sem((8,)),
            sem((NP,)),
            sem((NP,)),
            sem((2, 2, 5)),
            sem((2, 2, 5)),
            sem((2, 5, NP)),
            sem((2, 5, NP)),
            sem((2, QBLK, 2, 2)),
            sem((2, QBLK, 2, 2)),
            sem((2, QBLK, NX)),
            sem((2, QBLK, NX)),
            sem((QBLK + 1, NX)),
            sem((QBLK + 1, NX)),
            sem((NX, QBLK)),
            sem((NX, QBLK)),
            sem((3, NP)),
            sem((3, NP)),
            sem((NZ,)),
            sem((NZ,)),
            sem((2, NX)),
            sem((2, NX)),
        ],
        compiler_params=pltpu.CompilerParams(
            collective_id=0, has_side_effects=True, vmem_limit_bytes=58 << 20
        ),
        name="indexer_kl",
    )(
        block_ids,
        cache_latent.T,
        cache_index.reshape(8, NX, QROWS, IDIM),
        stretch_latent.T,
        stretch_index.reshape(QBLK, NX, QROWS, IDIM),
        jnp.transpose(query_latent, (1, 2, 0)),
        query_index,
        index_gains.T,
    )
    divergence, qgrad, ggrad, cache_grad, own_grad = pl.pallas_call(
        emit_kernel,
        out_shape=shapes,
        in_specs=[any_space] * 5,
        out_specs=(any_space,) * 5,
        scratch_shapes=[*[V(a.shape, a.dtype) for a in shapes], sem((2, 5))],
        compiler_params=pltpu.CompilerParams(vmem_limit_bytes=58 << 20),
        name="emit",
    )(*results)
    return (
        divergence.reshape(ROWS),
        qgrad,
        ggrad.T,
        cache_grad.reshape(CACHED, IDIM),
        own_grad.reshape(ROWS, IDIM),
    )


def solution(mesh):
    placed = (
        P("seq", "head", None),
        P("seq", None),
        P("seq", None),
        P("seq", "head", None),
        P("seq", None),
        P("seq", None),
        P("seq", "head"),
        P("seq", None),
    )
    return jax.shard_map(
        per_device,
        mesh=mesh,
        in_specs=placed,
        out_specs=(
            P("seq"),
            P("seq", "head", None),
            P("seq", "head"),
            P("seq", None),
            P("seq", None),
        ),
        check_vma=False,
    )
```

```python
import jax
import jax.numpy as jnp
from jax import lax
from jax.experimental import pallas as pl
from jax.experimental.pallas import tpu as pltpu
from jax.sharding import PartitionSpec as P

MESH = pl.DeviceIdType.MESH
HEADS = 128
SCORE_SCALE = 192.0 ** (-0.5)
LOG2E = 1.4426950408889634
BLK = 64
LAG = 2
PICKED = 7
QBLK = 4
NX = 4
NZ = 8
NP = 8
QROWS = BLK // NX
KDIM = 576
IDIM = 128
SPAN = 512
HEAD_A = 256
WIDE_A, WIDE_B = IDIM + HEAD_A, KDIM - HEAD_A
OCT = 8
LOCAL_HEADS = 32
NOCT = LOCAL_HEADS // OCT
IHEADS = 16
PART = 16
ROWS = QBLK * BLK
CACHED = 512


def z_place(offset):
    return jnp.where(offset == 0, 0, jnp.where(offset <= 4, 2 * offset - 1, 2 * (8 - offset)))


def place_offset(place):
    return jnp.where(place % 2 == 1, (place + 1) // 2, NZ - place // 2)


def kernel(ids, cl, ci, sl, si, q, qi_h, gains_h, out_div, out_qgrad, out_ggrad, out_cache, out_own, *scratch):
    refs = list(scratch)
    take = lambda n: [refs.pop(0) for _ in range(n)]
    stock_a, stock_b = take(NZ), take(NZ)
    send_a, send_b, recv_a, recv_b, key_a, key_b, want_v, want_s = take(8)
    cl_v, sl_v, q_v, qr, qi, gains = take(6)
    sums, mass_o, mass_b, logits, rs_m, rs_l, lg, div = take(8)
    kgrad, kquarter, kpart, krecv, slots, ret_s, ret_r, z_part, z_got, cache_g, own_g = take(11)
    ggrad_t, qgrad_v, ggrad_v, div_v = take(4)
    load_sem, q_sem, out_sem, ids_send, ids_recv, zs_send, zs_recv, ys_send, ys_recv = take(9)
    xs_send, xs_recv, rs_send, rs_recv, lg_send, lg_recv, k_send, k_recv = take(8)
    y_send, y_recv, z_send, z_recv, f_send, f_recv = take(6)

    seq = lax.axis_index("seq")
    h = lax.axis_index("head")
    z, me = seq // NP, seq % NP
    z_next, z_prev = ((z + 1) % NZ) * NP + me, ((z + NZ - 1) % NZ) * NP + me
    x_next, x_prev = (h + 1) % NX, (h + NX - 1) % NX
    quarter = pl.ds(pl.multiple_of(h * QROWS, QROWS), QROWS)

    def remote(src, dst, send, recv, target):
        return pltpu.make_async_remote_copy(
            src_ref=src,
            dst_ref=dst,
            send_sem=send,
            recv_sem=recv,
            device_id=target,
            device_id_type=MESH,
        )

    def each(count, copies, act):
        def body(i, _):
            for copy in copies(i):
                act(copy)
            return 0

        lax.fori_loop(1, count, body, 0)

    start = lambda copy: copy.start()
    wait = lambda copy: copy.wait()
    wait_recv = lambda copy: copy.wait_recv()
    wait_send = lambda copy: copy.wait_send()

    load_cl = pltpu.make_async_copy(cl, cl_v, load_sem.at[0])
    load_ci = pltpu.make_async_copy(ci.at[:, h], stock_a[0].at[:, :, pl.ds(0, IDIM)], load_sem.at[1])
    load_sl = pltpu.make_async_copy(sl, sl_v, load_sem.at[2])
    load_si = pltpu.make_async_copy(
        si, key_a.at[:, PICKED, :, :, pl.ds(0, IDIM)], load_sem.at[3]
    )
    load_qi = pltpu.make_async_copy(qi_h, qi, load_sem.at[4])
    load_gains = pltpu.make_async_copy(gains_h, gains, load_sem.at[5])
    load_q = [
        pltpu.make_async_copy(
            q.at[pl.ds(o * OCT, OCT)], q_v.at[pl.ds(o * OCT, OCT)], q_sem.at[o]
        )
        for o in range(NOCT)
    ]
    for load in [load_cl, load_ci, load_sl, load_si, *load_q, load_qi, load_gains]:
        load.start()

    barrier = pltpu.get_barrier_semaphore()

    def greet(count, target):
        def body(i, _):
            pl.semaphore_signal(barrier, inc=1, device_id=target(i), device_id_type=MESH)
            return 0

        lax.fori_loop(1, count, body, 0)

    greet(NZ, lambda i: (((z + i) % NZ) * NP + me, h))
    greet(NP, lambda i: (z * NP + (me + i) % NP, h))
    greet(NX, lambda i: (seq, (h + i) % NX))

    lane = lax.broadcasted_iota(jnp.int32, (8, 128), 1)
    row = lax.broadcasted_iota(jnp.int32, (8, 128), 0)
    tile = jnp.full((8, 128), -1, jnp.int32)
    for r in range(QBLK):
        for j in range(PICKED):
            block = ids[r, j]
            owner = block >> 3
            spot = (owner & 7) * NZ + z_place(((owner >> 3) - z + NZ) & 7)
            value = jnp.where(row == 0, block & 7, r * 8 + j)
            tile = jnp.where(lane == spot, value, tile)
    want_v[me] = tile

    load_cl.wait()
    for b in range(8):
        if b % 2 == 0:
            pair = cl_v[:, b * BLK : (b + 2) * BLK].T
        rows = pair[(b % 2) * BLK : (b % 2 + 1) * BLK].reshape(NX, QROWS, KDIM)
        mine = jnp.where(
            h == 0, rows[0], jnp.where(h == 1, rows[1], jnp.where(h == 2, rows[2], rows[3]))
        )
        stock_a[0][b, :, IDIM:] = mine[:, :HEAD_A]
        stock_b[0][b] = mine[:, HEAD_A:]
    load_ci.wait()
    pl.semaphore_wait(barrier, NX - 1 + NP - 1 + NZ - 1)

    def ids_copies(i):
        peer = (me + i) % NP
        return [
            remote(want_v.at[me], want_v.at[me], ids_send.at[i], ids_recv.at[i], (z * NP + peer, h))
        ]

    def zs_copy(a, step, way):
        stock = stock_b if a else stock_a
        if way == 0:
            src, dst = 2 * (step - 1), 2 * step if step < 4 else 7
            part, target = pl.ds(0, 4), z_next
        else:
            src, dst = max(2 * step - 3, 0), 2 * step - 1
            part, target = pl.ds(4, 4), z_prev
        if step < 4:
            part = pl.ds(0, 8)
        return remote(
            stock[src].at[part],
            stock[dst].at[part],
            zs_send.at[a, way, step],
            zs_recv.at[a, way, step],
            (target, h),
        )

    spans = ((0, 1), (1, 2), (3, 2), (5, 2), (7, 1))

    def ys_copy(a, step, i):
        first, count = spans[step]
        peer = (me + i) % NP
        send, recv = (send_b, recv_b) if a else (send_a, recv_a)
        return remote(
            send.at[peer, pl.ds(first, count)],
            recv.at[me, pl.ds(first, count)],
            ys_send.at[a, step, i],
            ys_recv.at[a, step, i],
            (z * NP + peer, h),
        )

    def stage(a, step):
        first, count = spans[step]
        stock, send, recv = (stock_b, send_b, recv_b) if a else (stock_a, send_a, recv_a)

        def body(i, _):
            peer = (me + i) % NP
            for p in range(first, first + count):
                block = jnp.maximum(want_s[peer, 0, me * NZ + p], 0)
                send[peer, p] = stock[p][block]
            ys_copy(a, step, i).start()
            return 0

        lax.fori_loop(1, NP, body, 0)
        for p in range(first, first + count):
            block = jnp.maximum(want_s[me, 0, me * NZ + p], 0)
            recv[me, p] = stock[p][block]

    def turn(a, step):
        for way in range(2):
            zs_copy(a, step, way).wait_recv()
            if step < 4:
                zs_copy(a, step + 1, way).start()

    def arrange(unit):
        p, o = unit % 2, unit // 2
        if p == 0:
            load_q[o].wait()
        for half in range(2):
            cut = slice(p * 128 + half * BLK, p * 128 + (half + 1) * BLK)
            qr[p * 2 + half, o] = jnp.concatenate(
                [q_v[o * OCT + i, :, cut] for i in range(OCT)], axis=1
            )

    def gathered(a):
        for step in range(len(spans)):
            each(NP, lambda i: [ys_copy(a, step, i)], wait)
        key, recv = (key_b, recv_b) if a else (key_a, recv_a)
        for r in range(QBLK):
            for j in range(PICKED):
                owner = ids[r, j] >> 3
                place = z_place(((owner >> 3) - z + NZ) & 7)
                key[r, j, h] = recv[owner & 7, place]

    def xs_copy(a, r, step, way):
        if step == 0:
            rows, part = h, pl.ds(0, PICKED)
        elif way == 0:
            rows, part = x_prev, pl.ds(0, 3 + r % 2)
        else:
            rows, part = x_next, pl.ds(3 + r % 2, 4 - r % 2)
        spot = (key_b if a else key_a).at[r, part, rows]
        return remote(
            spot,
            spot,
            xs_send.at[a, r, step, way],
            xs_recv.at[a, r, step, way],
            (seq, x_prev if way else x_next),
        )

    def xs_start(a, r):
        for way in range(2):
            xs_copy(a, r, 0, way).start()

    def xs_turn(a, r):
        for way in range(2):
            xs_copy(a, r, 0, way).wait_recv()
        for way in range(2):
            xs_copy(a, r, 1, way).start()

    def xs_done(a, r):
        for way in range(2):
            xs_copy(a, r, 1, way).wait_recv()

    def z_start(a):
        for way in range(2):
            zs_copy(a, 1, way).start()

    z_start(0)
    each(NP, ids_copies, start)
    load_sl.wait()
    for p in range(2):
        rows = sl_v[:, p * 128 : (p + 1) * 128].T
        for half in range(2):
            own = rows[half * BLK : (half + 1) * BLK].reshape(NX, QROWS, KDIM)
            key_a[2 * p + half, PICKED, :, :, IDIM:] = own[:, :, :HEAD_A]
            key_b[2 * p + half, PICKED] = own[:, :, HEAD_A:]
    arrange(0)
    each(NP, ids_copies, wait)
    to_scalar = pltpu.make_async_copy(want_v, want_s, load_sem.at[6])
    to_scalar.start()
    to_scalar.wait()
    stage(0, 0)
    for step in range(1, 5 + LAG):
        if step <= 4:
            turn(0, step)
        if step == LAG:
            z_start(1)
            stage(1, 0)
        if step <= 4:
            stage(0, step)
            if step == 4:
                gathered(0)
                for r in range(QBLK):
                    xs_start(0, r)
        if step > LAG:
            turn(1, step - LAG)
            stage(1, step - LAG)
            if step > 4:
                xs_turn(0, step - 5)
        if step <= 4:
            arrange(step)
    load_si.wait()
    gathered(1)
    xs_start(1, 0)
    for r in range(LAG, QBLK):
        xs_turn(0, r)
        xs_start(1, r - LAG + 1)

    def rs_copies(r, i):
        peer = (h + i) % NX
        theirs = pl.ds(pl.multiple_of(peer * QROWS, QROWS), QROWS)
        return [
            remote(
                src.at[r, theirs], dst.at[r, h], rs_send.at[a, r, i], rs_recv.at[a, r, i], (seq, peer)
            )
            for a, (src, dst) in enumerate(((logits, rs_l), (mass_b, rs_m)))
        ]

    def ikeys_of(r):
        return key_a[r, :, :, :, :IDIM].reshape(SPAN, IDIM)

    def gain_of(r, first):
        half = gains[:, (r // 2) * 128 : (r // 2 + 1) * 128]
        return pltpu.roll(half, 128 - (r % 2) * BLK - first, 1)

    def make_logits(r):
        ikeys = ikeys_of(r)

        def body(c, _):
            first = pl.multiple_of(c * PART, PART)
            iblock = qi[pl.ds(r * BLK + first, PART)].reshape(PART * IHEADS, IDIM)
            inner = lax.dot_general(
                iblock, ikeys, (((1,), (1,)), ((), ())), preferred_element_type=jnp.float32
            )
            gain = gain_of(r, first)
            rows = []
            for t in range(PART):
                live = jnp.maximum(inner[t * IHEADS : (t + 1) * IHEADS], 0.0)
                rows.append(jnp.sum(live * gain[:, t : t + 1], axis=0, keepdims=True))
            logits[r, pl.ds(first, PART)] = jnp.concatenate(rows, axis=0)
            return 0

        lax.fori_loop(0, BLK // PART, body, 0)

    def make_mass(r):
        keys = jnp.concatenate(
            [
                key_a[r, :, :, :, IDIM:].reshape(SPAN, HEAD_A),
                key_b[r].reshape(SPAN, WIDE_B),
            ],
            axis=1,
        )
        cut = PICKED * BLK
        scale = SCORE_SCALE * LOG2E
        own_row = lax.broadcasted_iota(jnp.int32, (BLK, OCT * BLK), 0)
        token = lax.broadcasted_iota(jnp.int32, (BLK, OCT * BLK), 1) % BLK
        allowed = own_row <= token
        sums[...] = jnp.zeros_like(sums)

        def body(o, _):
            scores = jnp.dot(keys, qr[r, o], preferred_element_type=jnp.float32)
            old, own = scores[:cut], jnp.where(allowed, scores[cut:], -jnp.inf)
            top = jnp.maximum(
                jnp.max(old, axis=0, keepdims=True), jnp.max(own, axis=0, keepdims=True)
            )
            e_old = jnp.exp2((old - top) * scale)
            e_own = jnp.exp2((own - top) * scale)
            total = jnp.sum(e_old, axis=0, keepdims=True) + jnp.sum(e_own, axis=0, keepdims=True)
            share = 1.0 / total
            for lo, hi, e in ((0, cut, e_old), (cut, SPAN, e_own)):
                part = e * share
                fold = part[:, :128]
                for i in range(1, OCT // 2):
                    fold = fold + part[:, i * 128 : (i + 1) * 128]
                sums[lo:hi] += fold
            return 0

        lax.fori_loop(0, NOCT, body, 0, unroll=NOCT)
        mass = (sums[:, :BLK] + sums[:, BLK:]).T

        mass_o[r] = mass
        mass_b[r] = mass.astype(jnp.bfloat16)
        each(NX, lambda i: rs_copies(r, i), start)

    def lg_copies(r, i):
        peer = (h + i) % NX
        return [remote(lg.at[r, quarter], lg.at[r, quarter], lg_send.at[r, i], lg_recv.at[r, i], (seq, peer))]

    def div_copies(i):
        peer = (h + i) % NX
        return [remote(div.at[h], div.at[h], lg_send.at[QBLK, i], lg_recv.at[QBLK, i], (seq, peer))]

    def divergence_of(r):
        each(NX, lambda i: rs_copies(r, i), wait)
        mass_sum, logit = mass_o[r, quarter], logits[r, quarter]
        for i in range(1, NX):
            mass_sum = mass_sum + rs_m[r, (h + i) % NX].astype(jnp.float32)
            logit = logit + rs_l[r, (h + i) % NX]
        target = mass_sum * (1.0 / HEADS)
        column = lax.broadcasted_iota(jnp.int32, (QROWS, SPAN), 1)
        token = lax.broadcasted_iota(jnp.int32, (QROWS, SPAN), 0) + h * QROWS
        allowed = column - PICKED * BLK <= token
        masked = jnp.where(allowed, logit, -jnp.inf)
        shifted = masked - jnp.max(masked, axis=1, keepdims=True)
        powers = jnp.exp(shifted)
        total = jnp.sum(powers, axis=1, keepdims=True)
        model = powers / total
        lg[r, quarter] = jnp.where(allowed, model - target, 0.0).astype(jnp.bfloat16)
        each(NX, lambda i: lg_copies(r, i), start)
        log_model = jnp.where(allowed, shifted - jnp.log(total), 0.0)
        safe = jnp.where(target > 0, target, 1.0)
        pointwise = jnp.where(allowed, target * (jnp.log(safe) - log_model), 0.0)
        divergence = jnp.sum(pointwise, axis=1, keepdims=True)
        spot = lax.broadcasted_iota(jnp.int32, (QROWS, 128), 1) == h * QROWS + (
            lax.broadcasted_iota(jnp.int32, (QROWS, 128), 0)
        )
        in_lanes = jnp.sum(jnp.where(spot, divergence, 0.0), axis=0, keepdims=True)
        return jnp.where(lax.broadcasted_iota(jnp.int32, (8, 128), 0) == r, in_lanes, 0.0)

    def k_copy(i, r):
        peer = (h + i) % NX
        return remote(
            kpart.at[r, :, peer], krecv.at[h, r], k_send.at[i, r], k_recv.at[i, r], (seq, peer)
        )

    def qgrad_copy(r):
        rows = pl.ds(r * BLK, BLK)
        return pltpu.make_async_copy(qgrad_v.at[rows], out_qgrad.at[rows], out_sem.at[r])

    stores = [
        pltpu.make_async_copy(src, dst, out_sem.at[QBLK + n])
        for n, (src, dst) in enumerate(
            ((ggrad_v, out_ggrad), (div_v, out_div), (own_g, out_own), (cache_g, out_cache))
        )
    ]

    def backward(r):
        each(NX, lambda i: lg_copies(r, i), wait)
        ikeys = ikeys_of(r)
        kgrad[...] = jnp.zeros_like(kgrad)
        ggrad_t[...] = jnp.zeros_like(ggrad_t)

        def body(c, _):
            first = pl.multiple_of(c * PART, PART)
            rows = pl.ds(r * BLK + first, PART)
            iblock = qi[rows].reshape(PART * IHEADS, IDIM)
            inner = lax.dot_general(
                iblock, ikeys, (((1,), (1,)), ((), ())), preferred_element_type=jnp.float32
            )
            slope = lg[r, pl.ds(first, PART)].astype(jnp.float32)
            gain = gain_of(r, first)
            lanes = lax.broadcasted_iota(jnp.int32, (IHEADS, 128), 1)
            found = jnp.zeros((IHEADS, 128), jnp.float32)
            grads = []
            for t in range(PART):
                piece = inner[t * IHEADS : (t + 1) * IHEADS]
                push = slope[t : t + 1]
                gsum = jnp.sum(jnp.maximum(piece, 0.0) * push, axis=1, keepdims=True)
                found = jnp.where(lanes == first + t, gsum, found)
                grads.append(
                    jnp.where(piece > 0, push * gain[:, t : t + 1], 0.0).astype(jnp.bfloat16)
                )
            ggrad_t[...] += found
            inner_grad = jnp.concatenate(grads, axis=0)
            qgrad = jnp.dot(inner_grad, ikeys, preferred_element_type=jnp.float32)
            qgrad_v[rows] = qgrad.astype(jnp.bfloat16).reshape(PART, IHEADS, IDIM)
            kgrad[...] += lax.dot_general(
                inner_grad, iblock, (((0,), (0,)), ((), ())), preferred_element_type=jnp.float32
            )
            return 0

        lax.fori_loop(0, BLK // PART, body, 0)
        for j in range(8):
            block = kgrad[pl.ds(j * BLK, BLK)].reshape(NX, QROWS, IDIM)
            kpart[r, j] = block.astype(jnp.bfloat16)
            kquarter[r, j] = kgrad[pl.ds(pl.multiple_of(j * BLK + h * QROWS, QROWS), QROWS)]
        each(NX, lambda i: [k_copy(i, r)], start)
        qgrad_copy(r).start()
        ggrad_v[:, r * BLK : (r + 1) * BLK] = ggrad_t[:, :BLK]

    load_qi.wait()
    load_gains.wait()
    for r in range(QBLK):
        xs_done(0, r)
        make_logits(r)
        if r < QBLK - 1:
            arrange(5 + r)
            xs_turn(1, r)
            if r + QBLK - LAG + 1 < QBLK:
                xs_start(1, r + QBLK - LAG + 1)
    tiles = []
    for r in range(QBLK):
        xs_done(1, r)
        make_mass(r)
        if r == 0:
            xs_turn(1, QBLK - 1)
        if r >= 1:
            tiles.append(divergence_of(r - 1))
        if r >= 2:
            backward(r - 2)
    tiles.append(divergence_of(QBLK - 1))
    div[h] = sum(tiles[1:], tiles[0])
    each(NX, div_copies, start)
    backward(QBLK - 2)
    backward(QBLK - 1)

    for r in range(QBLK):
        each(NX, lambda i: [k_copy(i, r)], wait)
        total = kquarter[r]
        for i in range(1, NX):
            total = total + krecv[(h + i) % NX, r].astype(jnp.float32)
        own_g[r, h] = total[PICKED]
        slots[pl.ds(r * 8, 8)] = total.astype(jnp.bfloat16)

    stores[0].start()

    def put_back(p, _):
        for place in range(NZ):
            slot = jnp.maximum(want_s[me, 1, p * NZ + place], 0)
            ret_s[p, place] = slots[slot]
        return 0

    lax.fori_loop(0, NP, put_back, 0)

    groups = ((5, 3), (3, 2), (0, 3))

    def y_copies(g, i):
        peer = (me + i) % NP
        places = pl.ds(groups[g][0], groups[g][1])
        return [
            remote(
                ret_s.at[peer, places],
                ret_r.at[me, places],
                y_send.at[g, i],
                y_recv.at[g, i],
                (z * NP + peer, h),
            )
        ]

    for g in range(3):
        each(NP, lambda i: y_copies(g, i), start)

    def own_copies(i):
        peer = (h + i) % NX
        return [remote(own_g.at[:, h], own_g.at[:, h], f_send.at[0, i], f_recv.at[0, i], (seq, peer))]

    each(NX, own_copies, start)
    ret_r[me] = ret_s[me]

    def z_copies(place):
        peer = ((z + place_offset(place)) % NZ) * NP + me
        return [remote(z_part.at[place], z_got.at[place], z_send.at[place], z_recv.at[place], (peer, h))]

    def add_up(place, _):
        sums8 = [jnp.zeros((QROWS, IDIM), jnp.float32) for _ in range(8)]
        for p in range(NP):
            block = want_s[p, 0, me * NZ + place]
            got = ret_r[p, place].astype(jnp.float32)
            for b in range(8):
                sums8[b] = sums8[b] + jnp.where(block == b, got, 0.0)
        for b in range(8):
            z_part[place, b] = sums8[b].astype(jnp.bfloat16)

        @pl.when(place > 0)
        def _():
            for copy in z_copies(place):
                copy.start()

        return 0

    for g, (first, count) in enumerate(groups):
        each(NP, lambda i: y_copies(g, i), wait)
        lax.fori_loop(0, count, lambda i, _: add_up(first + count - 1 - i, 0), 0)

    for step in range(1, 5):
        for way in range(2):
            for a in range(2):
                zs_copy(a, step, way).wait_send()
    for a in range(2):
        for r in range(QBLK):
            for step in range(2):
                for way in range(2):
                    xs_copy(a, r, step, way).wait_send()
    each(NX, div_copies, wait)
    spread = div[0] + div[1] + div[2] + div[3]
    for p in range(2):
        div_v[p : p + 1] = jnp.concatenate(
            [spread[2 * p : 2 * p + 1, :BLK], spread[2 * p + 1 : 2 * p + 2, :BLK]], axis=1
        )
    stores[1].start()
    each(NX, own_copies, wait)
    stores[2].start()
    each(NZ, z_copies, wait)
    cache_sum = z_part[0].astype(jnp.float32)
    for place in range(1, NZ):
        cache_sum = cache_sum + z_got[place].astype(jnp.float32)
    cache_g[:, h] = cache_sum

    def cache_copies(i):
        peer = (h + i) % NX
        return [
            remote(cache_g.at[:, h], cache_g.at[:, h], f_send.at[1, i], f_recv.at[1, i], (seq, peer))
        ]

    each(NX, cache_copies, start)
    each(NX, cache_copies, wait)
    stores[3].start()
    for r in range(QBLK):
        qgrad_copy(r).wait()
    for store in stores:
        store.wait()


def emit_kernel(*refs):
    ins, outs, held, sems = refs[:5], refs[5:10], refs[10:15], refs[15]
    order = (1, 3, 4, 2, 0)
    loads = [pltpu.make_async_copy(ins[n], held[n], sems.at[0, n]) for n in range(5)]
    stores = [pltpu.make_async_copy(held[n], outs[n], sems.at[1, n]) for n in range(5)]
    for n in order:
        loads[n].start()
    for n in order:
        loads[n].wait()
        stores[n].start()
    for n in order:
        stores[n].wait()


def per_device(
    query_latent,
    stretch_latent,
    cache_latent,
    query_index,
    stretch_index,
    cache_index,
    index_gains,
    block_ids,
):
    f32, bf16, sem, V = jnp.float32, jnp.bfloat16, pltpu.SemaphoreType.DMA, pltpu.VMEM
    any_space = pl.BlockSpec(memory_space=pltpu.HBM)
    shapes = (
        jax.ShapeDtypeStruct((2, 128), f32),
        jax.ShapeDtypeStruct((ROWS, IHEADS, IDIM), bf16),
        jax.ShapeDtypeStruct((IHEADS, ROWS), f32),
        jax.ShapeDtypeStruct((8, NX, QROWS, IDIM), f32),
        jax.ShapeDtypeStruct((QBLK, NX, QROWS, IDIM), f32),
    )
    results = pl.pallas_call(
        kernel,
        out_shape=shapes,
        in_specs=[pl.BlockSpec(memory_space=pltpu.SMEM)] + [any_space] * 7,
        out_specs=(any_space,) * 5,
        scratch_shapes=[
            *[V((8, QROWS, WIDE_A), bf16)] * NZ,
            *[V((8, QROWS, WIDE_B), bf16)] * NZ,
            V((NP, NZ, QROWS, WIDE_A), bf16),
            V((NP, NZ, QROWS, WIDE_B), bf16),
            V((NP, NZ, QROWS, WIDE_A), bf16),
            V((NP, NZ, QROWS, WIDE_B), bf16),
            V((QBLK, 8, NX, QROWS, WIDE_A), bf16),
            V((QBLK, 8, NX, QROWS, WIDE_B), bf16),
            V((NP, 8, 128), jnp.int32),
            pltpu.SMEM((NP, 8, 128), jnp.int32),
            V((KDIM, CACHED), bf16),
            V((KDIM, ROWS), bf16),
            V((LOCAL_HEADS, KDIM, ROWS), bf16),
            V((QBLK, NOCT, KDIM, OCT * BLK), bf16),
            V((ROWS, IHEADS, IDIM), bf16),
            V((IHEADS, ROWS), f32),
            V((SPAN, 128), f32),
            V((QBLK, BLK, SPAN), f32),
            V((QBLK, BLK, SPAN), bf16),
            V((QBLK, BLK, SPAN), f32),
            V((QBLK, NX, QROWS, SPAN), bf16),
            V((QBLK, NX, QROWS, SPAN), f32),
            V((QBLK, BLK, SPAN), bf16),
            V((QBLK, 8, 128), f32),
            V((SPAN, IDIM), f32),
            V((QBLK, 8, QROWS, IDIM), f32),
            V((QBLK, 8, NX, QROWS, IDIM), bf16),
            V((NX, QBLK, 8, QROWS, IDIM), bf16),
            V((QBLK * 8, QROWS, IDIM), bf16),
            V((NP, NZ, QROWS, IDIM), bf16),
            V((NP, NZ, QROWS, IDIM), bf16),
            V((NZ, 8, QROWS, IDIM), bf16),
            V((NZ, 8, QROWS, IDIM), bf16),
            V((8, NX, QROWS, IDIM), f32),
            V((QBLK, NX, QROWS, IDIM), f32),
            V((IHEADS, 128), f32),
            V((ROWS, IHEADS, IDIM), bf16),
            V((IHEADS, ROWS), f32),
            V((2, 128), f32),
            sem((7,)),
            sem((NOCT,)),
            sem((8,)),
            sem((NP,)),
            sem((NP,)),
            sem((2, 2, 5)),
            sem((2, 2, 5)),
            sem((2, 5, NP)),
            sem((2, 5, NP)),
            sem((2, QBLK, 2, 2)),
            sem((2, QBLK, 2, 2)),
            sem((2, QBLK, NX)),
            sem((2, QBLK, NX)),
            sem((QBLK + 1, NX)),
            sem((QBLK + 1, NX)),
            sem((NX, QBLK)),
            sem((NX, QBLK)),
            sem((3, NP)),
            sem((3, NP)),
            sem((NZ,)),
            sem((NZ,)),
            sem((2, NX)),
            sem((2, NX)),
        ],
        compiler_params=pltpu.CompilerParams(
            collective_id=0, has_side_effects=True, vmem_limit_bytes=58 << 20
        ),
        name="indexer_kl",
    )(
        block_ids,
        cache_latent.T,
        cache_index.reshape(8, NX, QROWS, IDIM),
        stretch_latent.T,
        stretch_index.reshape(QBLK, NX, QROWS, IDIM),
        jnp.transpose(query_latent, (1, 2, 0)),
        query_index,
        index_gains.T,
    )
    divergence, qgrad, ggrad, cache_grad, own_grad = pl.pallas_call(
        emit_kernel,
        out_shape=shapes,
        in_specs=[any_space] * 5,
        out_specs=(any_space,) * 5,
        scratch_shapes=[*[V(a.shape, a.dtype) for a in shapes], sem((2, 5))],
        compiler_params=pltpu.CompilerParams(vmem_limit_bytes=58 << 20),
        name="emit",
    )(*results)
    return (
        divergence.reshape(ROWS),
        qgrad,
        ggrad.T,
        cache_grad.reshape(CACHED, IDIM),
        own_grad.reshape(ROWS, IDIM),
    )


def solution(mesh):
    placed = (
        P("seq", "head", None),
        P("seq", None),
        P("seq", None),
        P("seq", "head", None),
        P("seq", None),
        P("seq", None),
        P("seq", "head"),
        P("seq", None),
    )
    return jax.shard_map(
        per_device,
        mesh=mesh,
        in_specs=placed,
        out_specs=(
            P("seq"),
            P("seq", "head", None),
            P("seq", "head"),
            P("seq", None),
            P("seq", None),
        ),
        check_vma=False,
    )
```
